256 devices in a mesh: rcv: 16 (over z_hi, y, core), shot: 16 (over z_lo, x).
Axes of the slice: x: 4, y: 4, z: 8 (z_hi: 2, z_lo: 4; z = z_hi * 4 + z_lo), core: 2. Of those that a mesh axis runs over, the one named last changes fastest.
Arguments:
- wavefield: bfloat16 [2, 2, 8192, 4096], P(None, None, 'shot', 'rcv'), may hold values from -6 to 6
Outputs:
- psf: float32 [2, 2, 4096, 4096], P(None, None, 'rcv', 'shot')
The draws below stay inside these ranges and needn't reach their ends.
All inputs are finite; a program needn't handle non-finite values.
Results may differ from the reference program's by a relative error of at most 0.0003.
Values may be sent and summed in bfloat16 or wider, within the bound.
No kernel may reach another device: no remote copies, remote signals or barrier semaphores. Data moves between devices by JAX's collectives and lax.ppermute only.
A program may use at most 192 MiB of HBM per device.

```python
import jax
import jax.numpy as jnp
from jax import lax

R = 4096
FREQS = 2
SHOTS = 8192


def raised(result, own_key, source, target, blocks, factor):
    def block_of(position):
        return (jnp.arange(result.shape[position]) // (result.shape[position] // blocks)).reshape((-1,) + (1,) * (result.ndim - 1 - position))

    near = jax.random.permutation(own_key, blocks)[block_of(target)]
    other_side = (block_of(target) + blocks // 2) % blocks
    return jnp.where((block_of(source) == near) | (block_of(source) == other_side), factor * result, result)


def block_levels(own_key, shape, cuts, low, high):
    def one(dim, shards_of):
        draws = jax.random.uniform(jax.random.fold_in(jax.random.fold_in(own_key, 6), dim), (shards_of,), jnp.float32, low / len(cuts), high / len(cuts))
        return jnp.repeat(jnp.exp(draws), shape[dim] // shards_of).reshape((-1,) + (1,) * (len(shape) - dim - 1))

    gain = one(*cuts[0])
    for cut in cuts[1:]:
        gain = gain * one(*cut)
    return gain


def gaussian_with(key, extent, deviation, reach, shards, heavy, held_as=jnp.bfloat16):
    values = deviation * jax.random.normal(key, extent, jnp.float32)
    if shards:
        values = values * block_levels(key, extent, shards, -0.22, 0.18)
    return jnp.clip(raised(values, jax.random.fold_in(key, 3), *heavy), -reach, reach).astype(held_as)


def setup_inputs(seed: int = 0) -> dict:
    key_list = jax.random.split(jax.random.key(seed), 2)
    return {
        "wavefield": gaussian_with(key_list[0], (FREQS, 2, SHOTS, R), 1.0, 6.0, ((2, 16), (3, 16)), (2, 3, 16, 2.0)),
    }


def reference(wavefield):
    scale = 1.0 / jnp.sqrt(jnp.float32(SHOTS))
    outs = []
    for f in range(FREQS):
        a = wavefield[f, 0].astype(jnp.float32)
        b = wavefield[f, 1].astype(jnp.float32)
        hi = lax.Precision.HIGHEST
        real_part = jnp.dot(a.T, a, precision=hi) + jnp.dot(b.T, b, precision=hi)
        imag_part = jnp.dot(a.T, b, precision=hi) - jnp.dot(b.T, a, precision=hi)
        outs.append(jnp.stack([real_part * scale, imag_part * scale]))
    return jnp.stack(outs)
```

```python
import itertools

import jax
import jax.numpy as jnp
import numpy as np
from jax import lax
from jax.sharding import Mesh
from jax.sharding import PartitionSpec as P

AXES = ("zh", "y", "core", "zl", "x")
SIZES = (2, 4, 2, 4, 4)
BLOCKS = 4


def rcv_of(zh, y, core):
    return (zh * 4 + y) * 2 + core


def device_of(row, col):
    return row * 16 + col


def z_of(row, col):
    return (row // 8) * 4 + col // 4


def held_pair(f, y, core, x, block):
    e_col, core_col = x // 2, x % 2
    if block < 2:
        e_row, dy = block, 1
    elif block == 2:
        e_row, dy = (e_col if y < 2 else 1 - e_col), 2
    else:
        if core_col == core:
            return None
        e_row, dy = (e_col if core == 0 else 1 - e_col), 0
    return rcv_of(f ^ e_row, y, core), rcv_of(f ^ e_col, (y + dy) % 4, core_col)


def deliveries(f, y, core, x, block):
    pair = held_pair(f, y, core, x, block)
    if pair is not None:
        row, col = pair
        plain, flipped = device_of(row, col), device_of(col, row)
        first, second = (plain, flipped) if f == 0 else (flipped, plain)
        return [(0, first), (1, first), (2, second), (3, second)]
    e_col = x // 2
    r0, r1 = rcv_of(0, y, core), rcv_of(1, y, core)
    own = rcv_of(f ^ e_col, y, core)
    d01, d10 = device_of(r0, r1), device_of(r1, r0)
    diag = device_of(own, own)
    if f == 0:
        return [(0, diag), (1, d01 if e_col == 0 else d10), (2, d10 if e_col == 0 else d01)]
    return [(1, diag), (0, d01 if e_col == 0 else d10), (3, d10 if e_col == 0 else d01)]


def ring_distance(a, b):
    d = (a - b) % 8
    return min(d, 8 - d)


def tables():
    slot_block = np.zeros((2, 4, 2, 4, 4), np.int32)
    perms = [[], [], [], []]
    for f, y, core, x in itertools.product(range(2), range(4), range(2), range(4)):
        costs = np.zeros((4, 4))
        for block in range(BLOCKS):
            for _, target in deliveries(f, y, core, x, block):
                z = z_of(target // 16, target % 16)
                for zl in range(4):
                    costs[zl, block] += ring_distance(4 * f + zl, z)
        best = min(itertools.permutations(range(4)), key=lambda p: sum(costs[zl, p[zl]] ** 2 for zl in range(4)))
        slot_block[f, y, core, x] = best
        for zl in range(4):
            source = device_of(rcv_of(f, y, core), zl * 4 + x)
            for slot, target in deliveries(f, y, core, x, best[zl]):
                perms[slot].append((source, target))
    for perm in perms:
        assert len({s for s, _ in perm}) == len(perm) == len({t for _, t in perm})
    case = np.zeros((16, 16), np.int32)
    for f, y, core, x, block in itertools.product(range(2), range(4), range(2), range(4), range(BLOCKS)):
        pair = held_pair(f, y, core, x, block)
        if pair is not None and f == 0:
            case[pair] = 1
    for y, core in itertools.product(range(4), range(2)):
        r0, r1 = rcv_of(0, y, core), rcv_of(1, y, core)
        case[r0, r0] = case[r1, r1] = 2
        case[r0, r1], case[r1, r0] = 3, 4
    return slot_block, perms, case


def ring(n, step):
    return [(i, (i + step) % n) for i in range(n)]


def gather_x(block):
    half = block.shape[1] // 2
    above = lax.ppermute(block, "x", ring(4, -1))
    below = lax.ppermute(block, "x", ring(4, 1))
    far_a = lax.ppermute(above[:, :half], "x", ring(4, -1))
    far_b = lax.ppermute(below[:, half:], "x", ring(4, 1))
    return jnp.concatenate([block, above, below, far_a, far_b], axis=1)


def from_core(mine, core_perm):
    return lax.ppermute(mine, ("core", "x"), core_perm)


def both_products(rows, cols):
    real = jnp.einsum("psm,psn->mn", rows, cols, preferred_element_type=jnp.float32)
    turned = jnp.stack([cols[1], -cols[0]])
    imag = jnp.einsum("psm,psn->mn", rows, turned, preferred_element_type=jnp.float32)
    return real, imag


def body(wavefield):
    slot_block, perms, case_of = tables()
    f, y, core, zl, x = (lax.axis_index(name) for name in AXES)
    n = wavefield.shape[3]
    shots = wavefield.shape[2] * 16
    scale = 1.0 / jnp.sqrt(jnp.float32(shots))

    own = lax.dynamic_index_in_dim(wavefield, f, 0, keepdims=False)
    other = lax.dynamic_index_in_dim(wavefield, 1 - f, 0, keepdims=False)
    other = lax.ppermute(other, "zh", ring(2, 1))
    block0, block1 = gather_x(own), gather_x(other)

    e_col, core_col = x // 2, x % 2
    mine = jnp.where(e_col == 0, block0, block1)
    one_way = [(a * 4 + b, (1 - a) * 4 + b) for a in range(2) for b in range(4) if b % 2 == a]
    cols0 = jnp.where(core_col == core, mine, from_core(mine, one_way))
    part = lax.dynamic_index_in_dim(cols0, core, 0, keepdims=False)
    swap = ring(2, 1)

    def from_y(step):
        near = lax.ppermute(part, "y", ring(4, -step))
        far = lax.ppermute(near, "core", swap)
        return jnp.where(core == 0, jnp.stack([near, far]), jnp.stack([far, near]))

    cols1, cols2 = from_y(1), from_y(2)

    rows = jnp.concatenate([block0, block1], axis=2)
    real1, imag1 = both_products(rows, cols1)
    e_row2 = jnp.where(y < 2, e_col, 1 - e_col)
    real2, imag2 = both_products(jnp.where(e_row2 == 0, block0, block1), cols2)
    real0, imag0 = both_products(rows, cols0)

    def rows_of(a, e):
        return lax.dynamic_slice_in_dim(a, e * n, n, 0)

    same = core_col == core
    e_row0 = jnp.where(same, 1 - e_col, jnp.where(core == 0, e_col, 1 - e_col))
    upper = lax.broadcasted_iota(jnp.int32, (n, n), 0) <= lax.broadcasted_iota(jnp.int32, (n, n), 1)
    packed = jnp.where(upper, rows_of(real0, e_col), rows_of(imag0, e_col))
    off_real, off_imag = rows_of(real0, e_row0), rows_of(imag0, e_row0)
    first0 = jnp.where(same, packed, off_real)
    second0 = jnp.where(same & (e_col == 0), off_real, off_imag)
    blocks = jnp.stack(
        [
            jnp.stack([real1[:n], imag1[:n]]),
            jnp.stack([real1[n:], imag1[n:]]),
            jnp.stack([real2, imag2]),
            jnp.stack([first0, second0]),
        ]
    )

    order = jnp.asarray(slot_block)[f, y, core, x]

    def partial_of(slot):
        return lax.dynamic_index_in_dim(blocks, order[jnp.clip(slot, 0, 3)], 0, keepdims=False)

    up = down = None
    for step in (1, 2, 3):
        send_up, send_down = partial_of(zl + 4 - step), partial_of(zl - 4 + step)
        if up is not None:
            send_up, send_down = send_up + up, send_down + down
        up = lax.ppermute(send_up, "zl", [(i, i + 1) for i in range(step)])
        down = lax.ppermute(send_down, "zl", [(3 - i, 2 - i) for i in range(step)])
    held = (partial_of(zl) + up + down) * scale

    plain_a, plain_b = held[0], held[1]
    turned_a, turned_b = held[0].T, -held[1].T
    special = same & (order[zl] == 3)
    other_turned = jnp.where(e_col == 0, held[1].T, turned_b)
    is0 = f == 0
    send = [
        jnp.where(is0, plain_a, jnp.where(special, plain_b, turned_a)),
        jnp.where(is0, jnp.where(special, other_turned, plain_b), jnp.where(special, plain_a, turned_b)),
        jnp.where(is0, jnp.where(special, plain_b, turned_a), plain_a),
        jnp.where(is0, turned_b, jnp.where(special, other_turned, plain_b)),
    ]
    got = [lax.ppermute(s, AXES, perm) for s, perm in zip(send, perms)]

    case = jnp.asarray(case_of)[rcv_of(f, y, core), zl * 4 + x]

    def unpack(packed):
        strict = lax.broadcasted_iota(jnp.int32, (n, n), 0) < lax.broadcasted_iota(jnp.int32, (n, n), 1)
        top, low = jnp.where(upper, packed, 0.0), jnp.where(upper, 0.0, packed)
        return top + jnp.where(strict, packed, 0.0).T, low - low.T

    real_d0, imag_d0 = unpack(got[0])
    real_d1, imag_d1 = unpack(got[1])

    def pick(plain, flipped, diag, d01, d10):
        return jnp.where(
            case == 0, flipped, jnp.where(case == 1, plain, jnp.where(case == 2, diag, jnp.where(case == 3, d01, d10)))
        )

    a1, b1, a2, b2 = got
    return jnp.stack(
        [
            jnp.stack([pick(a1, a2, real_d0, b1, a2), pick(b1, b2, imag_d0, a2, b1)]),
            jnp.stack([pick(a2, a1, real_d1, a1, b2), pick(b2, b1, imag_d1, b2, a1)]),
        ]
    )


def solution(mesh):
    fine = Mesh(mesh.devices.reshape(SIZES), AXES)
    return jax.shard_map(
        body,
        mesh=fine,
        in_specs=(P(None, None, ("zl", "x"), ("zh", "y", "core")),),
        out_specs=P(None, None, ("zh", "y", "core"), ("zl", "x")),
        check_vma=False,
    )
```

```python
import itertools

import jax
import jax.numpy as jnp
import numpy as np
from jax import lax
from jax.sharding import Mesh
from jax.sharding import PartitionSpec as P

AXES = ("zh", "y", "core", "zl", "x")
SIZES = (2, 4, 2, 4, 4)
BLOCKS = 4


def rcv_of(zh, y, core):
    return (zh * 4 + y) * 2 + core


def device_of(row, col):
    return row * 16 + col


def z_of(row, col):
    return (row // 8) * 4 + col // 4


def held_pair(f, y, core, x, block):
    e_col, core_col = x // 2, x % 2
    if block < 2:
        e_row, dy = block, 1
    elif block == 2:
        e_row, dy = (e_col if y < 2 else 1 - e_col), 2
    else:
        if core_col == core:
            return None
        e_row, dy = (e_col if core == 0 else 1 - e_col), 0
    return rcv_of(f ^ e_row, y, core), rcv_of(f ^ e_col, (y + dy) % 4, core_col)


def deliveries(f, y, core, x, block):
    pair = held_pair(f, y, core, x, block)
    if pair is not None:
        row, col = pair
        plain, flipped = device_of(row, col), device_of(col, row)
        first, second = (plain, flipped) if f == 0 else (flipped, plain)
        return [(0, first), (1, first), (2, second), (3, second)]
    e_col = x // 2
    r0, r1 = rcv_of(0, y, core), rcv_of(1, y, core)
    own = rcv_of(f ^ e_col, y, core)
    d01, d10 = device_of(r0, r1), device_of(r1, r0)
    diag = device_of(own, own)
    if f == 0:
        return [(0, diag), (1, d01 if e_col == 0 else d10), (2, d10 if e_col == 0 else d01)]
    return [(1, diag), (0, d01 if e_col == 0 else d10), (3, d10 if e_col == 0 else d01)]


def ring_distance(a, b):
    d = (a - b) % 8
    return min(d, 8 - d)


def tables():
    slot_block = np.zeros((2, 4, 2, 4, 4), np.int32)
    perms = [[], [], [], []]
    for f, y, core, x in itertools.product(range(2), range(4), range(2), range(4)):
        costs = np.zeros((4, 4))
        for block in range(BLOCKS):
            for _, target in deliveries(f, y, core, x, block):
                z = z_of(target // 16, target % 16)
                for zl in range(4):
                    costs[zl, block] += ring_distance(4 * f + zl, z)
        best = min(itertools.permutations(range(4)), key=lambda p: sum(costs[zl, p[zl]] ** 2 for zl in range(4)))
        slot_block[f, y, core, x] = best
        for zl in range(4):
            source = device_of(rcv_of(f, y, core), zl * 4 + x)
            for slot, target in deliveries(f, y, core, x, best[zl]):
                perms[slot].append((source, target))
    for perm in perms:
        assert len({s for s, _ in perm}) == len(perm) == len({t for _, t in perm})
    case = np.zeros((16, 16), np.int32)
    for f, y, core, x, block in itertools.product(range(2), range(4), range(2), range(4), range(BLOCKS)):
        pair = held_pair(f, y, core, x, block)
        if pair is not None and f == 0:
            case[pair] = 1
    for y, core in itertools.product(range(4), range(2)):
        r0, r1 = rcv_of(0, y, core), rcv_of(1, y, core)
        case[r0, r0] = case[r1, r1] = 2
        case[r0, r1], case[r1, r0] = 3, 4
    return slot_block, perms, case


def ring(n, step):
    return [(i, (i + step) % n) for i in range(n)]


def gather_x(block):
    half = block.shape[1] // 2
    above = lax.ppermute(block, "x", ring(4, -1))
    below = lax.ppermute(block, "x", ring(4, 1))
    far_a = lax.ppermute(above[:, :half], "x", ring(4, -1))
    far_b = lax.ppermute(below[:, half:], "x", ring(4, 1))
    return block, jnp.concatenate([above, below], axis=1), jnp.concatenate([far_a, far_b], axis=1)


def with_turned(real, imag):
    return jnp.stack([jnp.concatenate([real, imag], axis=1), jnp.concatenate([imag, -real], axis=1)])


def product(rows, cols):
    return jnp.einsum("psm,psn->mn", rows, cols, preferred_element_type=jnp.float32)


def body(wavefield):
    slot_block, perms, case_of = tables()
    f, y, core, zl, x = (lax.axis_index(name) for name in AXES)
    n = wavefield.shape[3]
    shots = wavefield.shape[2] * 16
    scale = 1.0 / jnp.sqrt(jnp.float32(shots))

    own = lax.dynamic_index_in_dim(wavefield, f, 0, keepdims=False)
    other = lax.dynamic_index_in_dim(wavefield, 1 - f, 0, keepdims=False)
    other = lax.ppermute(other, "zh", ring(2, 1))
    group0, group1 = gather_x(own), gather_x(other)

    e_col, core_col = x // 2, x % 2
    same = core_col == core
    e_row2 = jnp.where(y < 2, e_col, 1 - e_col)
    one_way = [(a * 4 + b, (1 - a) * 4 + b) for a in range(2) for b in range(4) if b % 2 == a]
    swap = ring(2, 1)
    product0 = product1 = product2 = 0.0

    def on_both(part):
        far = lax.ppermute(part, "core", swap)
        return with_turned(jnp.where(core == 0, part, far), jnp.where(core == 0, far, part))

    for group, (block0, block1) in enumerate(zip(group0, group1)):
        mine = jnp.where(e_col == 0, block0, block1)
        cols0 = jnp.where(same, mine, lax.ppermute(mine, ("core", "x"), one_way))
        part0 = lax.dynamic_index_in_dim(cols0, core, 0, keepdims=False)
        part1 = lax.ppermute(part0, "y", ring(4, -1))
        if group < 2:
            part2 = lax.ppermute(lax.ppermute(part0, "y", ring(4, 1)), "y", ring(4, 1))
        else:
            part2 = lax.ppermute(part1, "y", ring(4, -1))
        rows = jnp.concatenate([block0, block1], axis=2)
        product0 += product(rows, with_turned(cols0[0], cols0[1]))
        product1 += product(rows, on_both(part1))
        product2 += product(jnp.where(e_row2 == 0, block0, block1), on_both(part2))
    real0, imag0 = product0[:, :n], product0[:, n:]
    real1, imag1 = product1[:, :n], product1[:, n:]
    real2, imag2 = product2[:, :n], product2[:, n:]

    def rows_of(a, e):
        return lax.dynamic_slice_in_dim(a, e * n, n, 0)

    e_row0 = jnp.where(same, 1 - e_col, jnp.where(core == 0, e_col, 1 - e_col))
    upper = lax.broadcasted_iota(jnp.int32, (n, n), 0) <= lax.broadcasted_iota(jnp.int32, (n, n), 1)
    packed = jnp.where(upper, rows_of(real0, e_col), rows_of(imag0, e_col))
    off_real, off_imag = rows_of(real0, e_row0), rows_of(imag0, e_row0)
    first0 = jnp.where(same, packed, off_real)
    second0 = jnp.where(same & (e_col == 0), off_real, off_imag)
    blocks = jnp.stack(
        [
            jnp.stack([real1[:n], imag1[:n]]),
            jnp.stack([real1[n:], imag1[n:]]),
            jnp.stack([real2, imag2]),
            jnp.stack([first0, second0]),
        ]
    )

    order = jnp.asarray(slot_block)[f, y, core, x]

    def partial_of(slot):
        return lax.dynamic_index_in_dim(blocks, order[jnp.clip(slot, 0, 3)], 0, keepdims=False)

    up = down = None
    for step in (1, 2, 3):
        send_up, send_down = partial_of(zl + 4 - step), partial_of(zl - 4 + step)
        if up is not None:
            send_up, send_down = send_up + up, send_down + down
        up = lax.ppermute(send_up, "zl", [(i, i + 1) for i in range(step)])
        down = lax.ppermute(send_down, "zl", [(3 - i, 2 - i) for i in range(step)])
    held = (partial_of(zl) + up + down) * scale

    plain_a, plain_b = held[0], held[1]
    turned_a, turned_b = held[0].T, -held[1].T
    special = same & (order[zl] == 3)
    other_turned = jnp.where(e_col == 0, held[1].T, turned_b)
    is0 = f == 0
    send = [
        jnp.where(is0, plain_a, jnp.where(special, plain_b, turned_a)),
        jnp.where(is0, jnp.where(special, other_turned, plain_b), jnp.where(special, plain_a, turned_b)),
        jnp.where(is0, jnp.where(special, plain_b, turned_a), plain_a),
        jnp.where(is0, turned_b, jnp.where(special, other_turned, plain_b)),
    ]
    got = [lax.ppermute(s, AXES, perm) for s, perm in zip(send, perms)]

    case = jnp.asarray(case_of)[rcv_of(f, y, core), zl * 4 + x]

    def unpack(packed):
        strict = lax.broadcasted_iota(jnp.int32, (n, n), 0) < lax.broadcasted_iota(jnp.int32, (n, n), 1)
        top, low = jnp.where(upper, packed, 0.0), jnp.where(upper, 0.0, packed)
        return top + jnp.where(strict, packed, 0.0).T, low - low.T

    real_d0, imag_d0 = unpack(got[0])
    real_d1, imag_d1 = unpack(got[1])

    def pick(plain, flipped, diag, d01, d10):
        return jnp.where(
            case == 0, flipped, jnp.where(case == 1, plain, jnp.where(case == 2, diag, jnp.where(case == 3, d01, d10)))
        )

    a1, b1, a2, b2 = got
    return jnp.stack(
        [
            jnp.stack([pick(a1, a2, real_d0, b1, a2), pick(b1, b2, imag_d0, a2, b1)]),
            jnp.stack([pick(a2, a1, real_d1, a1, b2), pick(b2, b1, imag_d1, b2, a1)]),
        ]
    )


def solution(mesh):
    fine = Mesh(mesh.devices.reshape(SIZES), AXES)
    return jax.shard_map(
        body,
        mesh=fine,
        in_specs=(P(None, None, ("zl", "x"), ("zh", "y", "core")),),
        out_specs=P(None, None, ("zh", "y", "core"), ("zl", "x")),
        check_vma=False,
    )
```

```python
import itertools

import jax
import jax.numpy as jnp
import numpy as np
from jax import lax
from jax.sharding import Mesh
from jax.sharding import PartitionSpec as P

AXES = ("zh", "y", "core", "zl", "x")
SIZES = (2, 4, 2, 4, 4)
BLOCKS = 4


def rcv_of(zh, y, core):
    return (zh * 4 + y) * 2 + core


def device_of(row, col):
    return row * 16 + col


def z_of(row, col):
    return (row // 8) * 4 + col // 4


def held_pair(f, y, core, x, block):
    e_col, core_col = x // 2, x % 2
    if block < 2:
        e_row, dy = block, 1
    elif block == 2:
        e_row, dy = (e_col if y < 2 else 1 - e_col), 2
    else:
        if core_col == core:
            return None
        e_row, dy = (e_col if core == 0 else 1 - e_col), 0
    return rcv_of(f ^ e_row, y, core), rcv_of(f ^ e_col, (y + dy) % 4, core_col)


def deliveries(f, y, core, x, block):
    pair = held_pair(f, y, core, x, block)
    if pair is not None:
        row, col = pair
        plain, flipped = device_of(row, col), device_of(col, row)
        first, second = (plain, flipped) if f == 0 else (flipped, plain)
        return [(0, first), (1, first), (2, second), (3, second)]
    e_col = x // 2
    r0, r1 = rcv_of(0, y, core), rcv_of(1, y, core)
    own = rcv_of(f ^ e_col, y, core)
    d01, d10 = device_of(r0, r1), device_of(r1, r0)
    diag = device_of(own, own)
    if f == 0:
        return [(0, diag), (1, d01 if e_col == 0 else d10), (2, d10 if e_col == 0 else d01)]
    return [(1, diag), (0, d01 if e_col == 0 else d10), (3, d10 if e_col == 0 else d01)]


ROOTS = (
    (0x1d8a8f5a5b6d8927, 0xa0a990abf59a70e5),
    (0xf76030e586f052f8, 0x570e254e2c438e5b),
    (0x6758c4619e2552b9, 0x79d69d67e05aa158),
    (0x55aa8b65a45a9866, 0x65dea759bb55aa11),
)


def root_of(block, f, y, core, x):
    return ROOTS[block][f] >> (2 * (31 - ((y * 2 + core) * 4 + x))) & 3


def places():
    return itertools.product(range(2), range(4), range(2), range(4))


def sum_perms(block):
    perms = [[], [], []]
    for f, y, core, x in places():
        root = root_of(block, f, y, core, x)
        target = device_of(rcv_of(f, y, core), root * 4 + x)
        for back in (1, 2, 3):
            perms[back - 1].append((device_of(rcv_of(f, y, core), (root - back) % 4 * 4 + x), target))
    return perms


def owner_perms(block):
    perms = [[], [], [], []]
    for f, y, core, x in places():
        source = device_of(rcv_of(f, y, core), root_of(block, f, y, core, x) * 4 + x)
        for slot, target in deliveries(f, y, core, x, block):
            perms[slot].append((source, target))
    for perm in perms:
        assert len({s for s, _ in perm}) == len(perm) == len({t for _, t in perm})
    return perms


def owner_cases():
    case = np.zeros((16, 16), np.int32)
    for f, y, core, x in places():
        for block in range(BLOCKS):
            pair = held_pair(f, y, core, x, block)
            if pair is not None and f == 0:
                case[pair] = 1
    for y, core in itertools.product(range(4), range(2)):
        r0, r1 = rcv_of(0, y, core), rcv_of(1, y, core)
        case[r0, r0] = case[r1, r1] = 2
        case[r0, r1], case[r1, r0] = 3, 4
    return case


def ring(n, step):
    return [(i, (i + step) % n) for i in range(n)]


def gather_x(block):
    half = block.shape[1] // 2
    above = lax.ppermute(block, "x", ring(4, -1))
    below = lax.ppermute(block, "x", ring(4, 1))
    far_a = lax.ppermute(above[:, :half], "x", ring(4, -1))
    far_b = lax.ppermute(below[:, half:], "x", ring(4, 1))
    return block, jnp.concatenate([above, below], axis=1), jnp.concatenate([far_a, far_b], axis=1)


def with_turned(real, imag):
    return jnp.stack([jnp.concatenate([real, imag], axis=1), jnp.concatenate([imag, -real], axis=1)])


def first_of(value, *after):
    return lax.optimization_barrier((value, *after))[0] if after else value


def product(rows, cols):
    return jnp.einsum("psm,psn->mn", rows, cols, preferred_element_type=jnp.float32)


def body(wavefield):
    case_of = owner_cases()
    f, y, core, zl, x = (lax.axis_index(name) for name in AXES)
    n = wavefield.shape[3]
    shots = wavefield.shape[2] * 16
    scale = 1.0 / jnp.sqrt(jnp.float32(shots))

    own = lax.dynamic_index_in_dim(wavefield, f, 0, keepdims=False)
    other = lax.dynamic_index_in_dim(wavefield, 1 - f, 0, keepdims=False)
    other = lax.ppermute(other, "zh", ring(2, 1))
    group0, group1 = gather_x(own), gather_x(other)

    e_col, core_col = x // 2, x % 2
    same = core_col == core
    one_way = [(a * 4 + b, (1 - a) * 4 + b) for a in range(2) for b in range(4) if b % 2 == a]
    cols0, part = [], []
    for block0, block1 in zip(group0, group1):
        mine = jnp.where(e_col == 0, block0, block1)
        cols0.append(jnp.where(same, mine, lax.ppermute(mine, ("core", "x"), one_way)))
        part.append(lax.dynamic_index_in_dim(cols0[-1], core, 0, keepdims=False))

    def from_y(step, value, *after):
        return lax.ppermute(first_of(value, *after), "y", ring(4, -step))

    near, far = [None] * 3, [None] * 3
    near[0], far[0] = from_y(1, part[0]), from_y(2, part[0])
    near[1] = from_y(1, part[1], near[0], far[0])
    near[2] = from_y(1, part[2], near[1])
    far[1] = from_y(2, part[1], near[1])
    far[2] = from_y(2, part[2], near[2], far[1])

    def on_both(mine):
        other = lax.ppermute(mine, "core", ring(2, 1))
        return with_turned(jnp.where(core == 0, mine, other), jnp.where(core == 0, other, mine))

    rows = [jnp.concatenate(blocks, axis=2) for blocks in zip(group0, group1)]
    e_row2 = jnp.where(y < 2, e_col, 1 - e_col)
    rows2 = [jnp.where(e_row2 == 0, block0, block1) for block0, block1 in zip(group0, group1)]

    def parts_of(a):
        return jnp.stack([a[:, :n], a[:, n:]])

    product0 = sum(product(r, with_turned(c[0], c[1])) for r, c in zip(rows, cols0))
    e_row0 = jnp.where(same, 1 - e_col, jnp.where(core == 0, e_col, 1 - e_col))
    upper = lax.broadcasted_iota(jnp.int32, (n, n), 0) <= lax.broadcasted_iota(jnp.int32, (n, n), 1)
    diag = lax.dynamic_slice_in_dim(product0, e_col * n, n, 0)
    off = lax.dynamic_slice_in_dim(product0, e_row0 * n, n, 0)
    packed = jnp.where(upper, diag[:, :n], diag[:, n:])
    block3 = jnp.stack(
        [
            jnp.where(same, packed, off[:, :n]),
            jnp.where(same & (e_col == 0), off[:, :n], off[:, n:]),
        ]
    )

    def summed(block, number):
        return sum((lax.ppermute(block, AXES, perm) for perm in sum_perms(number)), block) * scale

    held3 = summed(block3, 3)
    product1 = sum(product(r, on_both(c)) for r, c in zip(rows, near))
    held0, held1 = summed(parts_of(product1[:n]), 0), summed(parts_of(product1[n:]), 1)
    cols2 = [on_both(c) for c in far]
    cols2[2] = first_of(cols2[2], held3)
    block2 = parts_of(sum(product(r, c) for r, c in zip(rows2, cols2)))
    held2 = summed(first_of(block2, held0, held1), 2)

    is0 = f == 0

    def turned(block):
        return jnp.stack([block[0].T, -block[1].T])

    firsts, seconds = [], []
    for number, held in ((0, held0), (1, held1), (2, held2)):
        perms = owner_perms(number)
        assert perms[0] == perms[1] and perms[2] == perms[3]
        firsts.append(lax.ppermute(jnp.where(is0, held, turned(held)), AXES, perms[0]))
        seconds.append(lax.ppermute(jnp.where(is0, turned(held), held), AXES, perms[2]))
    plain_a, plain_b = held3[0], held3[1]
    turned_a, turned_b = held3[0].T, -held3[1].T
    other_turned = jnp.where(e_col == 0, held3[1].T, turned_b)
    send = [
        jnp.where(is0, plain_a, jnp.where(same, plain_b, turned_a)),
        jnp.where(is0, jnp.where(same, other_turned, plain_b), jnp.where(same, plain_a, turned_b)),
        jnp.where(is0, jnp.where(same, plain_b, turned_a), plain_a),
        jnp.where(is0, turned_b, jnp.where(same, other_turned, plain_b)),
    ]
    last = [lax.ppermute(s, AXES, perm) for s, perm in zip(send, owner_perms(3))]
    first, second = sum(firsts), sum(seconds)
    got = [first[0] + last[0], first[1] + last[1], second[0] + last[2], second[1] + last[3]]

    case = jnp.asarray(case_of)[rcv_of(f, y, core), zl * 4 + x]

    def unpack(packed):
        strict = lax.broadcasted_iota(jnp.int32, (n, n), 0) < lax.broadcasted_iota(jnp.int32, (n, n), 1)
        top, low = jnp.where(upper, packed, 0.0), jnp.where(upper, 0.0, packed)
        return top + jnp.where(strict, packed, 0.0).T, low - low.T

    real_d0, imag_d0 = unpack(got[0])
    real_d1, imag_d1 = unpack(got[1])

    def pick(plain, flipped, diag, d01, d10):
        return jnp.where(
            case == 0, flipped, jnp.where(case == 1, plain, jnp.where(case == 2, diag, jnp.where(case == 3, d01, d10)))
        )

    a1, b1, a2, b2 = got
    return jnp.stack(
        [
            jnp.stack([pick(a1, a2, real_d0, b1, a2), pick(b1, b2, imag_d0, a2, b1)]),
            jnp.stack([pick(a2, a1, real_d1, a1, b2), pick(b2, b1, imag_d1, b2, a1)]),
        ]
    )


def solution(mesh):
    fine = Mesh(mesh.devices.reshape(SIZES), AXES)
    return jax.shard_map(
        body,
        mesh=fine,
        in_specs=(P(None, None, ("zl", "x"), ("zh", "y", "core")),),
        out_specs=P(None, None, ("zh", "y", "core"), ("zl", "x")),
        check_vma=False,
    )
```

```python
import itertools

import jax
import jax.numpy as jnp
import numpy as np
from jax import lax
from jax.sharding import Mesh
from jax.sharding import PartitionSpec as P

AXES = ("zh", "y", "core", "zl", "x")
SIZES = (2, 4, 2, 4, 4)
BLOCKS = 4


def rcv_of(zh, y, core):
    return (zh * 4 + y) * 2 + core


def device_of(row, col):
    return row * 16 + col


def places():
    return itertools.product(range(2), range(4), range(2), range(4))


def held_pair(f, y, core, x, block, core_col):
    e_col = x // 2
    if block < 2:
        e_row, dy = block, 1
    elif block == 2:
        e_row, dy = (e_col if y < 2 else 1 - e_col), 2
    elif core_col != core:
        e_row, dy = (e_col if core == 0 else 1 - e_col), 0
    elif e_col == f:
        return rcv_of(1, y, core), rcv_of(0, y, core)
    else:
        return None
    return rcv_of(f ^ e_row, y, core), rcv_of(f ^ e_col, (y + dy) % 4, core_col)


def deliveries(f, y, core, x, block):
    out = []
    for core_col in range(2):
        j = core_col ^ (x % 2)
        pair = held_pair(f, y, core, x, block, core_col)
        if pair is None:
            first, second = (device_of(r, r) for r in (rcv_of(f, y, core), rcv_of(1 - f, y, core)))
        else:
            first, second = device_of(*pair), device_of(*pair[::-1])
            if f == 1:
                first, second = second, first
        out += [(j, first), (2 + j, second)]
    return out


SLOTS = (
    (
        ((0x78, 0x93, 0x87, 0x4e), (0x72, 0xd8, 0x4e, 0x8d)),
        ((0xe1, 0x4e, 0x93, 0x63), (0xc9, 0x72, 0x8d, 0x4e)),
        ((0xb1, 0x87, 0x2d, 0x27), (0x93, 0xb1, 0x2d, 0x2d)),
        ((0x6c, 0x8d, 0x93, 0x2d), (0x93, 0x93, 0xe1, 0x2d)),
    ),
    (
        ((0x8d, 0x39, 0xb1, 0x4e), (0xc9, 0xe1, 0x72, 0x72)),
        ((0xb1, 0x2d, 0xd2, 0xd2), (0x8d, 0x39, 0xb1, 0x72)),
        ((0x36, 0xe1, 0x4e, 0x72), (0x39, 0xc6, 0xd2, 0x4e)),
        ((0xb1, 0xc6, 0x4e, 0x78), (0x1b, 0xb1, 0x9c, 0x4e)),
    ),
)


def slots_of(f, y, core, x):
    code = SLOTS[f][y][core][x]
    return [code >> (2 * zl) & 3 for zl in range(4)]


def tables():
    slots = np.zeros((2, 4, 2, 4, 4), np.int32)
    perms = [[], [], [], []]
    for f, y, core, x in places():
        slots[f, y, core, x] = slots_of(f, y, core, x)
        for zl in range(4):
            source = device_of(rcv_of(f, y, core), zl * 4 + x)
            for slot, target in deliveries(f, y, core, x, slots[f, y, core, x, zl]):
                perms[slot].append((source, target))
    for perm in perms:
        assert len({s for s, _ in perm}) == len(perm) == len({t for _, t in perm}) == 256
    case = np.zeros((16, 16), np.int32)
    for f, y, core, x in places():
        for block, core_col in itertools.product(range(BLOCKS), range(2)):
            pair = held_pair(f, y, core, x, block, core_col)
            if pair is not None and f == 0:
                case[pair] = 1
    for row in range(16):
        case[row, row] = 2
    return slots, perms, case


def ring(n, step):
    return [(i, (i + step) % n) for i in range(n)]


def gather_x(block):
    half = block.shape[1] // 2
    above = lax.ppermute(block, "x", ring(4, -1))
    below = lax.ppermute(block, "x", ring(4, 1))
    far_a = lax.ppermute(above[:, :half], "x", ring(4, -1))
    far_b = lax.ppermute(below[:, half:], "x", ring(4, 1))
    return jnp.concatenate([block, above, below, far_a, far_b], axis=1)


def dot(rows, cols):
    return lax.dot_general(rows, cols, (((0,), (0,)), ((), ())), preferred_element_type=jnp.float32)


def product(rows, cols):
    real = jnp.einsum("psm,psn->mn", rows, cols, preferred_element_type=jnp.float32)
    return jnp.stack([real, dot(rows[0], cols[1]) - dot(rows[1], cols[0])])


def body(wavefield):
    slots, perms, case_of = tables()
    f, y, core, zl, x = (lax.axis_index(name) for name in AXES)
    n = wavefield.shape[3]
    half = n // 2
    scale = 1.0 / jnp.sqrt(jnp.float32(wavefield.shape[2] * 16))
    e_col, h_col = x // 2, x % 2

    own = lax.dynamic_index_in_dim(wavefield, f, 0, keepdims=False)
    other = lax.dynamic_index_in_dim(wavefield, 1 - f, 0, keepdims=False)
    other = lax.ppermute(other, "zh", ring(2, 1))

    near = [lax.ppermute(block, "y", ring(4, -1)) for block in (own, other)]
    far = [lax.ppermute(block, "y", ring(4, -2)) for block in (own, other)]
    block0, block1 = gather_x(own), gather_x(other)

    def half_of(block, h):
        return jnp.where(h == 0, block[..., :half], block[..., half:])

    def quarter(pair, place):
        return half_of(jnp.where(place // 2 == 0, pair[0], pair[1]), place % 2)

    def quarters(place):
        return jnp.stack([quarter(near, place), quarter(far, place)])

    pieces = [quarters(x)]
    for step in (-1, 1, 2):
        pieces.append(lax.ppermute(quarters((x + step) % 4), "x", ring(4, step)))
    mine = jnp.concatenate(pieces, axis=2)

    def both(a, b):
        return jnp.where(core == 0, jnp.concatenate([a, b], -1), jnp.concatenate([b, a], -1))

    cols = both(mine, lax.ppermute(mine, "core", ring(2, 1)))
    mine0 = half_of(jnp.where(e_col == 0, block0, block1), h_col)
    other0 = lax.ppermute(mine0, "core", ring(2, 1))

    rows = jnp.concatenate([block0, block1], axis=2)
    upper = lax.broadcasted_iota(jnp.int32, (n, n), 0) <= lax.broadcasted_iota(jnp.int32, (n, n), 1)
    upper_half = half_of(upper, h_col)
    cross = product(jnp.where((e_col == 0) == (core == 0), block0, block1), other0)
    inner = product(rows, half_of(block0, h_col))
    inner1 = product(rows, half_of(block1, h_col))
    is0 = f == 0
    diag0, diag1 = jnp.where(is0, inner[:, :n], inner1[:, n:]), jnp.where(is0, inner1[:, n:], inner[:, :n])
    packed = jnp.stack([jnp.where(upper_half, d[0], d[1]) for d in (diag0, diag1)])
    block3 = both(jnp.where(e_col == f, jnp.where(is0, inner[:, n:], inner1[:, :n]), packed), cross)

    product1 = product(rows, cols[0])
    product2 = product(jnp.where((e_col == 0) == (y < 2), block0, block1), cols[1])
    blocks = jnp.stack([product1[:, :n], product1[:, n:], product2, block3])

    order = jnp.asarray(slots)[f, y, core, x]
    held = sum_over_zl(blocks, order, zl) * scale

    def part(j):
        return jnp.where((h_col ^ j) == 0, held[..., :half], held[..., half:])

    got = [lax.ppermute(part(slot % 2), AXES, perm) for slot, perm in enumerate(perms)]
    row, col = rcv_of(f, y, core), zl * 4 + x
    case = jnp.asarray(case_of)[row, col]
    swapped = jnp.where(case == 0, row, col) % 2 == 1

    def joined(a, b):
        return jnp.where(swapped, jnp.concatenate([b, a], -1), jnp.concatenate([a, b], -1))

    first, second = joined(got[0], got[1]), joined(got[2], got[3])

    def unpack(packed):
        strict = lax.broadcasted_iota(jnp.int32, (n, n), 0) < lax.broadcasted_iota(jnp.int32, (n, n), 1)
        top, low = jnp.where(upper, packed, 0.0), jnp.where(upper, 0.0, packed)
        return jnp.stack([top + jnp.where(strict, packed, 0.0).T, low - low.T])

    def turned(block):
        return jnp.stack([block[0].T, -block[1].T])

    diag_first, diag_second = (unpack(jnp.where(is0, a[0], a[1])) for a in (first, second))
    out0 = jnp.where(case == 1, first, jnp.where(case == 0, turned(second), jnp.where(is0, diag_first, diag_second)))
    out1 = jnp.where(case == 1, second, jnp.where(case == 0, turned(first), jnp.where(is0, diag_second, diag_first)))
    return jnp.stack([out0, out1])


def sum_over_zl(blocks, order, zl):
    def partial_of(slot):
        return lax.dynamic_index_in_dim(blocks, order[slot], 0, keepdims=False)

    total = partial_of(zl)
    for step in (1, 2, 3):
        total = total + lax.ppermute(partial_of((zl + step) % 4), "zl", ring(4, step))
    return total


def solution(mesh):
    fine = Mesh(mesh.devices.reshape(SIZES), AXES)
    return jax.shard_map(
        body,
        mesh=fine,
        in_specs=(P(None, None, ("zl", "x"), ("zh", "y", "core")),),
        out_specs=P(None, None, ("zh", "y", "core"), ("zl", "x")),
        check_vma=False,
    )
```

```python
import itertools

import jax
import jax.numpy as jnp
import numpy as np
from jax import lax
from jax.sharding import Mesh
from jax.sharding import PartitionSpec as P

AXES = ("zh", "y", "core", "zl", "x")
SIZES = (2, 4, 2, 4, 4)
BLOCKS = 4


def rcv_of(zh, y, core):
    return (zh * 4 + y) * 2 + core


def device_of(row, col):
    return row * 16 + col


def places():
    return itertools.product(range(2), range(4), range(2), range(4))


QUARTERS = (
    ((0, 1, 2, 3), (0, 1, 2, 3), (0, 2, 1, 3), (2, 0, 3, 1)),
    ((0, 1, 2, 3), (0, 1, 2, 3), (0, 2, 1, 3), (3, 1, 2, 0)),
)


def held_pair(f, y, core, x, block, core_col):
    e_quarter = QUARTERS[f][y][x] // 2
    e_col = e_quarter ^ core_col
    if block < 2:
        e_row, dy = block, 1
    elif block == 2:
        e_row, dy = e_quarter ^ core ^ (y // 2), 2
    elif core_col != core:
        e_row, dy = 1 - e_quarter, 0
    elif e_col == f:
        return rcv_of(1, y, core), rcv_of(0, y, core)
    else:
        return None
    return rcv_of(f ^ e_row, y, core), rcv_of(f ^ e_col, (y + dy) % 4, core_col)


def deliveries(f, y, core, x, block):
    out = []
    for core_col in range(2):
        j = core_col ^ (QUARTERS[f][y][x] % 2)
        pair = held_pair(f, y, core, x, block, core_col)
        if pair is None:
            first, second = (device_of(r, r) for r in (rcv_of(f, y, core), rcv_of(1 - f, y, core)))
        else:
            first, second = device_of(*pair), device_of(*pair[::-1])
            if f == 1:
                first, second = second, first
        out += [(j, first), (2 + j, second)]
    return out


SLOTS = (
    (
        ((0xe4, 0xb4, 0x4b, 0x4b), (0xc6, 0x4e, 0xe4, 0xe4)),
        ((0xe1, 0xe1, 0x87, 0x27), (0xc9, 0xc9, 0xe1, 0xd8)),
        ((0xb1, 0x2d, 0xb1, 0x2d), (0xe1, 0xc9, 0xe1, 0xc9)),
        ((0x9c, 0x93, 0x9c, 0x93), (0xc9, 0xe4, 0xe4, 0xe4)),
    ),
    (
        ((0xe1, 0xe1, 0x72, 0x72), (0x63, 0x63, 0x78, 0x78)),
        ((0xe1, 0xe1, 0x27, 0x39), (0x27, 0x27, 0xe1, 0xd8)),
        ((0xe1, 0xd2, 0xb1, 0xc6), (0x4e, 0xb1, 0x27, 0x93)),
        ((0x72, 0xc9, 0xe1, 0xe1), (0x8d, 0x6c, 0x93, 0x27)),
    ),
)


def slots_of(f, y, core, x):
    code = SLOTS[f][y][core][x]
    return [code >> (2 * zl) & 3 for zl in range(4)]


def tables():
    slots = np.zeros((2, 4, 2, 4, 4), np.int32)
    perms = [[], [], [], []]
    for f, y, core, x in places():
        slots[f, y, core, x] = slots_of(f, y, core, x)
        for zl in range(4):
            source = device_of(rcv_of(f, y, core), zl * 4 + x)
            for slot, target in deliveries(f, y, core, x, slots[f, y, core, x, zl]):
                perms[slot].append((source, target))
    for perm in perms:
        assert len({s for s, _ in perm}) == len(perm) == len({t for _, t in perm}) == 256
    case = np.zeros((16, 16), np.int32)
    for f, y, core, x in places():
        for block, core_col in itertools.product(range(BLOCKS), range(2)):
            pair = held_pair(f, y, core, x, block, core_col)
            if pair is not None and f == 0:
                case[pair] = 1
    for row in range(16):
        case[row, row] = 2
    return slots, perms, case


def ring(n, step):
    return [(i, (i + step) % n) for i in range(n)]


def gather_x(block):
    half = block.shape[1] // 2
    above = lax.ppermute(block, "x", ring(4, -1))
    below = lax.ppermute(block, "x", ring(4, 1))
    far_a = lax.ppermute(above[:, :half], "x", ring(4, -1))
    far_b = lax.ppermute(below[:, half:], "x", ring(4, 1))
    return jnp.concatenate([block, above, below, far_a, far_b], axis=1)


def dot(rows, cols):
    return lax.dot_general(rows, cols, (((0,), (0,)), ((), ())), preferred_element_type=jnp.float32)


def product(rows, cols):
    real = jnp.einsum("psm,psn->mn", rows, cols, preferred_element_type=jnp.float32)
    return jnp.stack([real, dot(rows[0], cols[1]) - dot(rows[1], cols[0])])


def body(wavefield):
    slots, perms, case_of = tables()
    f, y, core, zl, x = (lax.axis_index(name) for name in AXES)
    n = wavefield.shape[3]
    half = n // 2
    scale = 1.0 / jnp.sqrt(jnp.float32(wavefield.shape[2] * 16))
    quarter_at = jnp.asarray(QUARTERS, jnp.int32)[f, y]
    e_quarter, h_col = quarter_at[x] // 2, quarter_at[x] % 2
    e_col = e_quarter ^ core

    own = lax.dynamic_index_in_dim(wavefield, f, 0, keepdims=False)
    other = lax.dynamic_index_in_dim(wavefield, 1 - f, 0, keepdims=False)
    other = lax.ppermute(other, "zh", ring(2, 1))

    near = [lax.ppermute(block, "y", ring(4, -1)) for block in (own, other)]
    far = [lax.ppermute(block, "y", ring(4, -2)) for block in (own, other)]
    block0, block1 = gather_x(own), gather_x(other)

    def half_of(block, h):
        return jnp.where(h == 0, block[..., :half], block[..., half:])

    def quarter(pair, number):
        return half_of(jnp.where(number // 2 == core, pair[0], pair[1]), number % 2)

    def quarters(place):
        return jnp.stack([quarter(near, quarter_at[place]), quarter(far, quarter_at[place])])

    pieces = [quarters(x)]
    for step in (-1, 1, 2):
        pieces.append(lax.ppermute(quarters((x + step) % 4), "x", ring(4, step)))
    mine = jnp.concatenate(pieces, axis=2)

    def both(a, b):
        return jnp.where(core == 0, jnp.concatenate([a, b], -1), jnp.concatenate([b, a], -1))

    cols = both(mine, lax.ppermute(mine, "core", ring(2, 1)))
    mine0 = half_of(jnp.where(e_col == 0, block0, block1), h_col)
    other0 = lax.ppermute(mine0, "core", ring(2, 1))

    rows = jnp.concatenate([block0, block1], axis=2)
    upper = lax.broadcasted_iota(jnp.int32, (n, n), 0) <= lax.broadcasted_iota(jnp.int32, (n, n), 1)
    upper_half = half_of(upper, h_col)
    cross = product(jnp.where(e_quarter == 1, block0, block1), other0)
    inner = product(rows, half_of(block0, h_col))
    inner1 = product(rows, half_of(block1, h_col))
    is0 = f == 0
    diag0, diag1 = jnp.where(is0, inner[:, :n], inner1[:, n:]), jnp.where(is0, inner1[:, n:], inner[:, :n])
    packed = jnp.stack([jnp.where(upper_half, d[0], d[1]) for d in (diag0, diag1)])
    block3 = both(jnp.where(e_col == f, jnp.where(is0, inner[:, n:], inner1[:, :n]), packed), cross)

    product1 = product(rows, cols[0])
    product2 = product(jnp.where(e_col == y // 2, block0, block1), cols[1])
    blocks = jnp.stack([product1[:, :n], product1[:, n:], product2, block3])

    order = jnp.asarray(slots)[f, y, core, x]
    ordered = jnp.stack([lax.dynamic_index_in_dim(blocks, order[slot], 0, keepdims=False) for slot in range(BLOCKS)])
    held = lax.psum_scatter(ordered, "zl")
    held = held * scale

    def part(j):
        return jnp.where((h_col ^ j) == 0, held[..., :half], held[..., half:])

    got = [lax.ppermute(part(slot % 2), AXES, perm) for slot, perm in enumerate(perms)]
    row, col = rcv_of(f, y, core), zl * 4 + x
    case = jnp.asarray(case_of)[row, col]
    swapped = jnp.where(case == 0, row, col) % 2 == 1

    def joined(a, b):
        return jnp.where(swapped, jnp.concatenate([b, a], -1), jnp.concatenate([a, b], -1))

    first, second = joined(got[0], got[1]), joined(got[2], got[3])

    def unpack(packed):
        strict = lax.broadcasted_iota(jnp.int32, (n, n), 0) < lax.broadcasted_iota(jnp.int32, (n, n), 1)
        top, low = jnp.where(upper, packed, 0.0), jnp.where(upper, 0.0, packed)
        return jnp.stack([top + jnp.where(strict, packed, 0.0).T, low - low.T])

    def turned(block):
        return jnp.stack([block[0].T, -block[1].T])

    diag_first, diag_second = (unpack(jnp.where(is0, a[0], a[1])) for a in (first, second))
    out0 = jnp.where(case == 1, first, jnp.where(case == 0, turned(second), jnp.where(is0, diag_first, diag_second)))
    out1 = jnp.where(case == 1, second, jnp.where(case == 0, turned(first), jnp.where(is0, diag_second, diag_first)))
    return jnp.stack([out0, out1])


def solution(mesh):
    fine = Mesh(mesh.devices.reshape(SIZES), AXES)
    return jax.shard_map(
        body,
        mesh=fine,
        in_specs=(P(None, None, ("zl", "x"), ("zh", "y", "core")),),
        out_specs=P(None, None, ("zh", "y", "core"), ("zl", "x")),
        check_vma=False,
    )
```

```python
import itertools

import jax
import jax.numpy as jnp
import numpy as np
from jax import lax
from jax.sharding import Mesh
from jax.sharding import PartitionSpec as P

AXES = ("zh", "y", "core", "zl", "x")
SIZES = (2, 4, 2, 4, 4)
BLOCKS = 4


def rcv_of(zh, y, core):
    return (zh * 4 + y) * 2 + core


def device_of(row, col):
    return row * 16 + col


def places():
    return itertools.product(range(2), range(4), range(2), range(4))


QUARTERS = (
    ((0, 1, 2, 3), (0, 1, 2, 3), (0, 2, 1, 3), (2, 0, 3, 1)),
    ((0, 1, 2, 3), (0, 1, 2, 3), (0, 2, 1, 3), (3, 1, 2, 0)),
)


def held_pair(f, y, core, x, block, core_col):
    e_quarter = QUARTERS[f][y][x] // 2
    e_col = e_quarter ^ core_col
    if block < 2:
        e_row, dy = block, 1
    elif block == 2:
        e_row, dy = e_quarter ^ core ^ (y // 2), 2
    elif core_col != core:
        e_row, dy = 1 - e_quarter, 0
    elif e_col == f:
        return rcv_of(1, y, core), rcv_of(0, y, core)
    else:
        return None
    return rcv_of(f ^ e_row, y, core), rcv_of(f ^ e_col, (y + dy) % 4, core_col)


def deliveries(f, y, core, x, block):
    out = []
    for core_col in range(2):
        j = core_col ^ (QUARTERS[f][y][x] % 2)
        pair = held_pair(f, y, core, x, block, core_col)
        if pair is None:
            first, second = (device_of(r, r) for r in (rcv_of(f, y, core), rcv_of(1 - f, y, core)))
        else:
            first, second = device_of(*pair), device_of(*pair[::-1])
            if f == 1:
                first, second = second, first
        out += [(j, first), (2 + j, second)]
    return out


SLOTS = (
    (
        ((0xe4, 0xb4, 0x4b, 0x4b), (0xc6, 0x4e, 0xe4, 0xe4)),
        ((0xe1, 0xe1, 0x87, 0x27), (0xc9, 0xc9, 0xe1, 0xd8)),
        ((0xb1, 0x2d, 0xb1, 0x2d), (0xe1, 0xc9, 0xe1, 0xc9)),
        ((0x9c, 0x93, 0x9c, 0x93), (0xc9, 0xe4, 0xe4, 0xe4)),
    ),
    (
        ((0xe1, 0xe1, 0x72, 0x72), (0x63, 0x63, 0x78, 0x78)),
        ((0xe1, 0xe1, 0x27, 0x39), (0x27, 0x27, 0xe1, 0xd8)),
        ((0xe1, 0xd2, 0xb1, 0xc6), (0x4e, 0xb1, 0x27, 0x93)),
        ((0x72, 0xc9, 0xe1, 0xe1), (0x8d, 0x6c, 0x93, 0x27)),
    ),
)


def slots_of(f, y, core, x):
    code = SLOTS[f][y][core][x]
    return [code >> (2 * zl) & 3 for zl in range(4)]


def tables():
    slots = np.zeros((2, 4, 2, 4, 4), np.int32)
    perms = [[], [], [], []]
    for f, y, core, x in places():
        slots[f, y, core, x] = slots_of(f, y, core, x)
        for zl in range(4):
            source = device_of(rcv_of(f, y, core), zl * 4 + x)
            for slot, target in deliveries(f, y, core, x, slots[f, y, core, x, zl]):
                perms[slot].append((source, target))
    for perm in perms:
        assert len({s for s, _ in perm}) == len(perm) == len({t for _, t in perm}) == 256
    case = np.zeros((16, 16), np.int32)
    for f, y, core, x in places():
        for block, core_col in itertools.product(range(BLOCKS), range(2)):
            pair = held_pair(f, y, core, x, block, core_col)
            if pair is not None and f == 0:
                case[pair] = 1
    for row in range(16):
        case[row, row] = 2
    return slots, perms, case


def ring(n, step):
    return [(i, (i + step) % n) for i in range(n)]


def gather_x(block):
    half = block.shape[1] // 2
    above = lax.ppermute(block, "x", ring(4, -1))
    below = lax.ppermute(block, "x", ring(4, 1))
    far_a = lax.ppermute(above[:, :half], "x", ring(4, -1))
    far_b = lax.ppermute(below[:, half:], "x", ring(4, 1))
    return jnp.concatenate([block, above, below, far_a, far_b], axis=1)


def first_of(value, *after):
    return lax.optimization_barrier((value, *after))[0]


def product(rows, cols):
    n = cols.shape[2]
    turned = jnp.stack([jnp.concatenate([cols[0], cols[1]], -1), jnp.concatenate([cols[1], -cols[0]], -1)])
    both = jnp.einsum("psm,psn->mn", rows, turned, preferred_element_type=jnp.float32)
    return jnp.stack([both[:, :n], both[:, n:]])


def body(wavefield):
    slots, perms, case_of = tables()
    f, y, core, zl, x = (lax.axis_index(name) for name in AXES)
    n = wavefield.shape[3]
    half = n // 2
    scale = 1.0 / jnp.sqrt(jnp.float32(wavefield.shape[2] * 16))
    quarter_at = jnp.asarray(QUARTERS, jnp.int32)[f, y]
    e_quarter, h_col = quarter_at[x] // 2, quarter_at[x] % 2
    e_col = e_quarter ^ core

    other = lax.dynamic_index_in_dim(wavefield, 1 - f, 0, keepdims=False)
    own = lax.dynamic_index_in_dim(first_of(wavefield, other), f, 0, keepdims=False)
    other = lax.ppermute(other, "zh", ring(2, 1))

    near = [lax.ppermute(block, "y", ring(4, -1)) for block in (own, other)]
    far = [lax.ppermute(block, "y", ring(4, -2)) for block in (own, other)]
    block0, block1 = gather_x(own), gather_x(other)

    def half_of(block, h):
        return jnp.where(h == 0, block[..., :half], block[..., half:])

    def quarter(pair, number):
        return half_of(jnp.where(number // 2 == core, pair[0], pair[1]), number % 2)

    def quarters(place):
        return jnp.stack([quarter(near, quarter_at[place]), quarter(far, quarter_at[place])])

    pieces = [quarters(x)]
    for step in (-1, 1, 2):
        pieces.append(lax.ppermute(quarters((x + step) % 4), "x", ring(4, step)))
    mine = jnp.concatenate(pieces, axis=2)

    theirs = lax.ppermute(mine, "core", ring(2, 1))
    mine0 = half_of(jnp.where(e_col == 0, block0, block1), h_col)
    theirs0 = lax.ppermute(mine0, "core", ring(2, 1))

    rows = jnp.concatenate([block0, block1], axis=2)
    upper = lax.broadcasted_iota(jnp.int32, (n, n), 0) <= lax.broadcasted_iota(jnp.int32, (n, n), 1)
    upper_half = half_of(upper, h_col)
    cross = product(jnp.where(e_quarter == 1, block0, block1), theirs0)
    inner0 = product(rows, half_of(block0, h_col))
    inner1 = product(rows, half_of(block1, h_col))
    is0 = f == 0
    diag0, diag1 = jnp.where(is0, inner0[:, :n], inner1[:, n:]), jnp.where(is0, inner1[:, n:], inner0[:, :n])
    packed = jnp.stack([jnp.where(upper_half, d[0], d[1]) for d in (diag0, diag1)])
    inner = jnp.where(e_col == f, jnp.where(is0, inner0[:, n:], inner1[:, :n]), packed)

    rows2 = jnp.where(e_col == y // 2, block0, block1)
    order = jnp.asarray(slots)[f, y, core, x]
    arrived = []
    got = []
    for j in range(2):
        ours = (j ^ h_col) == core
        cols = jnp.where(ours, mine, theirs)
        product1 = product(rows, cols[0])
        blocks = jnp.stack(
            [product1[:, :n], product1[:, n:], product(rows2, cols[1]), jnp.where(ours, inner, cross)]
        )
        if j == 1:
            blocks = first_of(blocks, *arrived)

        def partial_of(slot, blocks=blocks):
            return lax.dynamic_index_in_dim(blocks, order[slot], 0, keepdims=False)

        arrived = [lax.ppermute(partial_of((zl + step) % 4), "zl", ring(4, step)) for step in (1, 2, 3)]
        held = (partial_of(zl) + arrived[0] + arrived[1] + arrived[2]) * scale
        got.append([lax.ppermute(held, AXES, perms[2 * kind + j]) for kind in range(2)])

    row, col = rcv_of(f, y, core), zl * 4 + x
    case = jnp.asarray(case_of)[row, col]
    swapped = jnp.where(case == 0, row, col) % 2 == 1

    def joined(a, b):
        return jnp.where(swapped, jnp.concatenate([b, a], -1), jnp.concatenate([a, b], -1))

    first, second = (joined(got[0][kind], got[1][kind]) for kind in range(2))

    def unpack(packed):
        strict = lax.broadcasted_iota(jnp.int32, (n, n), 0) < lax.broadcasted_iota(jnp.int32, (n, n), 1)
        top, low = jnp.where(upper, packed, 0.0), jnp.where(upper, 0.0, packed)
        return jnp.stack([top + jnp.where(strict, packed, 0.0).T, low - low.T])

    def turned(block):
        return jnp.stack([block[0].T, -block[1].T])

    diag_first, diag_second = (unpack(jnp.where(is0, a[0], a[1])) for a in (first, second))
    out0 = jnp.where(case == 1, first, jnp.where(case == 0, turned(second), jnp.where(is0, diag_first, diag_second)))
    out1 = jnp.where(case == 1, second, jnp.where(case == 0, turned(first), jnp.where(is0, diag_second, diag_first)))
    return jnp.stack([out0, out1])


def solution(mesh):
    fine = Mesh(mesh.devices.reshape(SIZES), AXES)
    return jax.shard_map(
        body,
        mesh=fine,
        in_specs=(P(None, None, ("zl", "x"), ("zh", "y", "core")),),
        out_specs=P(None, None, ("zh", "y", "core"), ("zl", "x")),
        check_vma=False,
    )
```

```python
import itertools

import jax
import jax.numpy as jnp
import numpy as np
from jax import lax
from jax.sharding import Mesh
from jax.sharding import PartitionSpec as P

AXES = ("zh", "y", "core", "zl", "x")
SIZES = (2, 4, 2, 4, 4)
BLOCKS = 4


def rcv_of(zh, y, core):
    return (zh * 4 + y) * 2 + core


def device_of(row, col):
    return row * 16 + col


def places():
    return itertools.product(range(2), range(4), range(2), range(4))


QUARTERS = (
    ((0, 1, 2, 3), (0, 1, 2, 3), (0, 2, 1, 3), (2, 0, 3, 1)),
    ((0, 1, 2, 3), (0, 1, 2, 3), (0, 2, 1, 3), (3, 1, 2, 0)),
)


def held_pair(f, y, core, x, block, core_col):
    e_quarter = QUARTERS[f][y][x] // 2
    e_col = e_quarter ^ core_col
    if block < 2:
        e_row, dy = block, 1
    elif block == 2:
        e_row, dy = e_quarter ^ core ^ (y // 2), 2
    elif core_col != core:
        e_row, dy = 1 - e_quarter, 0
    elif e_col == f:
        return rcv_of(1, y, core), rcv_of(0, y, core)
    else:
        return None
    return rcv_of(f ^ e_row, y, core), rcv_of(f ^ e_col, (y + dy) % 4, core_col)


def deliveries(f, y, core, x, block):
    out = []
    for core_col in range(2):
        j = core_col ^ (QUARTERS[f][y][x] % 2)
        pair = held_pair(f, y, core, x, block, core_col)
        if pair is None:
            first, second = (device_of(r, r) for r in (rcv_of(f, y, core), rcv_of(1 - f, y, core)))
        else:
            first, second = device_of(*pair), device_of(*pair[::-1])
            if f == 1:
                first, second = second, first
        out += [(j, first), (2 + j, second)]
    return out


SLOTS = (
    (
        ((0xe4, 0xb4, 0x4b, 0x4b), (0xc6, 0x4e, 0xe4, 0xe4)),
        ((0xe1, 0xe1, 0x87, 0x27), (0xc9, 0xc9, 0xe1, 0xd8)),
        ((0xb1, 0x2d, 0xb1, 0x2d), (0xe1, 0xc9, 0xe1, 0xc9)),
        ((0x9c, 0x93, 0x9c, 0x93), (0xc9, 0xe4, 0xe4, 0xe4)),
    ),
    (
        ((0xe1, 0xe1, 0x72, 0x72), (0x63, 0x63, 0x78, 0x78)),
        ((0xe1, 0xe1, 0x27, 0x39), (0x27, 0x27, 0xe1, 0xd8)),
        ((0xe1, 0xd2, 0xb1, 0xc6), (0x4e, 0xb1, 0x27, 0x93)),
        ((0x72, 0xc9, 0xe1, 0xe1), (0x8d, 0x6c, 0x93, 0x27)),
    ),
)


def slots_of(f, y, core, x):
    code = SLOTS[f][y][core][x]
    return [code >> (2 * zl) & 3 for zl in range(4)]


def tables():
    slots = np.zeros((2, 4, 2, 4, 4), np.int32)
    perms = [[], [], [], []]
    for f, y, core, x in places():
        slots[f, y, core, x] = slots_of(f, y, core, x)
        for zl in range(4):
            source = device_of(rcv_of(f, y, core), zl * 4 + x)
            for slot, target in deliveries(f, y, core, x, slots[f, y, core, x, zl]):
                perms[slot].append((source, target))
    for perm in perms:
        assert len({s for s, _ in perm}) == len(perm) == len({t for _, t in perm}) == 256
    case = np.zeros((16, 16), np.int32)
    for f, y, core, x in places():
        for block, core_col in itertools.product(range(BLOCKS), range(2)):
            pair = held_pair(f, y, core, x, block, core_col)
            if pair is not None and f == 0:
                case[pair] = 1
    for row in range(16):
        case[row, row] = 2
    return slots, perms, case


def ring(n, step):
    return [(i, (i + step) % n) for i in range(n)]


def gather_x(block):
    half = block.shape[1] // 2
    above = lax.ppermute(block, "x", ring(4, -1))
    below = lax.ppermute(block, "x", ring(4, 1))
    far_a = lax.ppermute(above[:, :half], "x", ring(4, -1))
    far_b = lax.ppermute(below[:, half:], "x", ring(4, 1))
    return jnp.concatenate([block, above, below, far_a, far_b], axis=1)


def first_of(value, *after):
    return lax.optimization_barrier((value, *after))[0]


def looked_up(values, index):
    out = jnp.uint32(values[0])
    for i in range(1, len(values)):
        out = jnp.where(index == i, jnp.uint32(values[i]), out)
    return out


def product(rows, cols):
    n = cols.shape[2]
    turned = jnp.stack([jnp.concatenate([cols[0], cols[1]], -1), jnp.concatenate([cols[1], -cols[0]], -1)])
    both = jnp.einsum("psm,psn->mn", rows, turned, preferred_element_type=jnp.float32)
    return jnp.stack([both[:, :n], both[:, n:]])


def body(wavefield):
    slots, perms, case_of = tables()
    slots = slots.reshape(64, 4) @ (1 << 2 * np.arange(4))
    f, y, core, zl, x = (lax.axis_index(name) for name in AXES)
    n = wavefield.shape[3]
    half = n // 2
    scale = 1.0 / jnp.sqrt(jnp.float32(wavefield.shape[2] * 16))
    quarter_code = looked_up([sum(q << 2 * i for i, q in enumerate(QUARTERS[i // 4][i % 4])) for i in range(8)], f * 4 + y)

    def quarter_at(place):
        return (quarter_code >> (2 * place).astype(jnp.uint32)).astype(jnp.int32) & 3

    e_quarter, h_col = quarter_at(x) // 2, quarter_at(x) % 2
    e_col = e_quarter ^ core

    other = lax.dynamic_index_in_dim(wavefield, 1 - f, 0, keepdims=False)
    own = lax.dynamic_index_in_dim(first_of(wavefield, other), f, 0, keepdims=False)
    other = lax.ppermute(other, "zh", ring(2, 1))

    block0 = gather_x(own)
    near = [lax.ppermute(own, "y", ring(4, -1)), lax.ppermute(other, "y", ring(4, -1))]
    far = [lax.ppermute(own, "y", ring(4, -2)), lax.ppermute(first_of(other, near[1]), "y", ring(4, -2))]
    block1 = gather_x(other)

    def half_of(block, h):
        return jnp.where(h == 0, block[..., :half], block[..., half:])

    def quarter(pair, number):
        return half_of(jnp.where(number // 2 == core, pair[0], pair[1]), number % 2)

    def to_quarters(pair, *after):
        pieces = [quarter(pair, quarter_at(x))]
        for step in (-1, 1, 2):
            piece = first_of(quarter(pair, quarter_at((x + step) % 4)), *after)
            pieces.append(lax.ppermute(piece, "x", ring(4, step)))
        return jnp.concatenate(pieces, axis=1)

    def from_core(piece):
        return lax.ppermute(piece, "core", ring(2, 1))

    mine1 = to_quarters(near)
    theirs1 = from_core(mine1)
    mine2 = to_quarters(far, mine1)
    theirs2 = from_core(mine2)
    mine0 = half_of(jnp.where(e_col == 0, block0, block1), h_col)
    theirs0 = from_core(mine0)

    rows = jnp.concatenate([block0, block1], axis=2)
    upper = lax.broadcasted_iota(jnp.int32, (n, n), 0) <= lax.broadcasted_iota(jnp.int32, (n, n), 1)
    upper_half = half_of(upper, h_col)
    cross = product(jnp.where(e_quarter == 1, block0, block1), theirs0)
    inner0 = product(rows, half_of(block0, h_col))
    inner1 = product(rows, half_of(block1, h_col))
    is0 = f == 0
    diag0, diag1 = jnp.where(is0, inner0[:, :n], inner1[:, n:]), jnp.where(is0, inner1[:, n:], inner0[:, :n])
    packed = jnp.stack([jnp.where(upper_half, d[0], d[1]) for d in (diag0, diag1)])
    inner = jnp.where(e_col == f, jnp.where(is0, inner0[:, n:], inner1[:, :n]), packed)

    rows2 = jnp.where(e_col == y // 2, block0, block1)
    order = looked_up(slots, ((f * 4 + y) * 2 + core) * 4 + x)
    arrived = []
    got = []
    for j in range(2):
        ours = (j ^ h_col) == core
        product1 = product(rows, jnp.where(ours, mine1, theirs1))
        product2 = product(rows2, jnp.where(ours, mine2, theirs2))
        blocks = jnp.stack([product1[:, :n], product1[:, n:], product2, jnp.where(ours, inner, cross)])
        if j == 1:
            blocks = first_of(blocks, *arrived)

        def partial_of(slot, blocks=blocks):
            return lax.dynamic_index_in_dim(blocks, (order >> (2 * slot).astype(jnp.uint32)).astype(jnp.int32) & 3, 0, keepdims=False)

        arrived = [lax.ppermute(partial_of((zl + step) % 4), "zl", ring(4, step)) for step in (1, 2, 3)]
        held = (partial_of(zl) + arrived[0] + arrived[1] + arrived[2]) * scale
        if j == 1:
            held = first_of(held, *got[0])
        got.append([lax.ppermute(held, AXES, perms[2 * kind + j]) for kind in range(2)])

    row, col = rcv_of(f, y, core), zl * 4 + x
    case = looked_up(case_of @ (1 << 2 * np.arange(16, dtype=np.int64)), row) >> (2 * col).astype(jnp.uint32) & 3
    swapped = jnp.where(case == 0, row, col) % 2 == 1

    def joined(a, b):
        return jnp.where(swapped, jnp.concatenate([b, a], -1), jnp.concatenate([a, b], -1))

    first, second = (joined(got[0][kind], got[1][kind]) for kind in range(2))

    def unpack(packed):
        strict = lax.broadcasted_iota(jnp.int32, (n, n), 0) < lax.broadcasted_iota(jnp.int32, (n, n), 1)
        top, low = jnp.where(upper, packed, 0.0), jnp.where(upper, 0.0, packed)
        return jnp.stack([top + jnp.where(strict, packed, 0.0).T, low - low.T])

    def turned(block):
        return jnp.stack([block[0].T, -block[1].T])

    diag_first, diag_second = (unpack(jnp.where(is0, a[0], a[1])) for a in (first, second))
    out0 = jnp.where(case == 1, first, jnp.where(case == 0, turned(second), jnp.where(is0, diag_first, diag_second)))
    out1 = jnp.where(case == 1, second, jnp.where(case == 0, turned(first), jnp.where(is0, diag_second, diag_first)))
    return jnp.stack([out0, out1])


def solution(mesh):
    fine = Mesh(mesh.devices.reshape(SIZES), AXES)
    return jax.shard_map(
        body,
        mesh=fine,
        in_specs=(P(None, None, ("zl", "x"), ("zh", "y", "core")),),
        out_specs=P(None, None, ("zh", "y", "core"), ("zl", "x")),
        check_vma=False,
    )
```

```python
import itertools

import jax
import jax.numpy as jnp
import numpy as np
from jax import lax
from jax.sharding import Mesh
from jax.sharding import PartitionSpec as P

AXES = ("zh", "y", "core", "zl", "x")
SIZES = (2, 4, 2, 4, 4)
BLOCKS = 4


def rcv_of(zh, y, core):
    return (zh * 4 + y) * 2 + core


def device_of(row, col):
    return row * 16 + col


def places():
    return itertools.product(range(2), range(4), range(2), range(4))


QUARTERS = (
    ((0, 1, 2, 3), (0, 1, 2, 3), (0, 2, 1, 3), (2, 0, 3, 1)),
    ((0, 1, 2, 3), (0, 1, 2, 3), (0, 2, 1, 3), (3, 1, 2, 0)),
)


def held_pair(f, y, core, x, block, core_col):
    e_quarter = QUARTERS[f][y][x] // 2
    e_col = e_quarter ^ core_col
    if block < 2:
        e_row, dy = block, 1
    elif block == 2:
        e_row, dy = e_quarter ^ core ^ (y // 2), 2
    elif core_col != core:
        e_row, dy = 1 - e_quarter, 0
    elif e_col == f:
        return rcv_of(1, y, core), rcv_of(0, y, core)
    else:
        return None
    return rcv_of(f ^ e_row, y, core), rcv_of(f ^ e_col, (y + dy) % 4, core_col)


def deliveries(f, y, core, x, block):
    out = []
    for core_col in range(2):
        j = core_col ^ (QUARTERS[f][y][x] % 2)
        pair = held_pair(f, y, core, x, block, core_col)
        if pair is None:
            first, second = (device_of(r, r) for r in (rcv_of(f, y, core), rcv_of(1 - f, y, core)))
        else:
            first, second = device_of(*pair), device_of(*pair[::-1])
            if f == 1:
                first, second = second, first
        out += [(j, first), (2 + j, second)]
    return out


SLOTS = (
    (
        ((0xe4, 0xb4, 0x4b, 0x4b), (0xc6, 0x4e, 0xe4, 0xe4)),
        ((0xe1, 0xe1, 0x87, 0x27), (0xc9, 0xc9, 0xe1, 0xd8)),
        ((0xb1, 0x2d, 0xb1, 0x2d), (0xe1, 0xc9, 0xe1, 0xc9)),
        ((0x9c, 0x93, 0x9c, 0x93), (0xc9, 0xe4, 0xe4, 0xe4)),
    ),
    (
        ((0xe1, 0xe1, 0x72, 0x72), (0x63, 0x63, 0x78, 0x78)),
        ((0xe1, 0xe1, 0x27, 0x39), (0x27, 0x27, 0xe1, 0xd8)),
        ((0xe1, 0xd2, 0xb1, 0xc6), (0x4e, 0xb1, 0x27, 0x93)),
        ((0x72, 0xc9, 0xe1, 0xe1), (0x8d, 0x6c, 0x93, 0x27)),
    ),
)


def slots_of(f, y, core, x):
    code = SLOTS[f][y][core][x]
    return [code >> (2 * zl) & 3 for zl in range(4)]


def tables():
    slots = np.zeros((2, 4, 2, 4, 4), np.int32)
    perms = [[], [], [], []]
    for f, y, core, x in places():
        slots[f, y, core, x] = slots_of(f, y, core, x)
        for zl in range(4):
            source = device_of(rcv_of(f, y, core), zl * 4 + x)
            for slot, target in deliveries(f, y, core, x, slots[f, y, core, x, zl]):
                perms[slot].append((source, target))
    for perm in perms:
        assert len({s for s, _ in perm}) == len(perm) == len({t for _, t in perm}) == 256
    case = np.zeros((16, 16), np.int32)
    for f, y, core, x in places():
        for block, core_col in itertools.product(range(BLOCKS), range(2)):
            pair = held_pair(f, y, core, x, block, core_col)
            if pair is not None and f == 0:
                case[pair] = 1
    for row in range(16):
        case[row, row] = 2
    return slots, perms, case


def ring(n, step):
    return [(i, (i + step) % n) for i in range(n)]


def gather_x(block):
    half = block.shape[1] // 2
    above = lax.ppermute(block, "x", ring(4, -1))
    below = lax.ppermute(block, "x", ring(4, 1))
    far_a = lax.ppermute(above[:, :half], "x", ring(4, -1))
    far_b = lax.ppermute(below[:, half:], "x", ring(4, 1))
    return [block, above, below, far_a, far_b]


def first_of(value, *after):
    return lax.optimization_barrier((value, *after))[0]


def looked_up(values, index):
    out = jnp.uint32(values[0])
    for i in range(1, len(values)):
        out = jnp.where(index == i, jnp.uint32(values[i]), out)
    return out


TOP = 12


def power_of(a):
    return jnp.clip(jnp.floor(jnp.log2(jnp.max(jnp.abs(a)))), -100.0, 100.0)


def pattern(shape):
    i, j = (lax.broadcasted_iota(jnp.int32, shape, axis) for axis in (1, 2))
    return ((i * 157 + j * 91) % 256 - 127.5).astype(jnp.float32) * 2.0**-18


def packed_half(a, power):
    scaled = a * (jnp.exp2(TOP - power) * (1.0 + pattern(a.shape)))
    rows = jnp.full((a.shape[0], 16, a.shape[2]), power)
    return jnp.concatenate([scaled, rows], axis=1).astype(jnp.float16)


def unpacked_half(a):
    values = a[:, :-16].astype(jnp.float32)
    power = a[0, -1, 0].astype(jnp.float32)
    return values * (jnp.exp2(power - TOP) * (1.0 - pattern(values.shape)))


def product(rows, cols):
    n = cols.shape[2]
    turned = jnp.stack([jnp.concatenate([cols[0], cols[1]], -1), jnp.concatenate([cols[1], -cols[0]], -1)])
    both = jnp.einsum("psm,psn->mn", rows, turned, preferred_element_type=jnp.float32)
    return jnp.stack([both[:, :n], both[:, n:]])


def body(wavefield):
    slots, perms, case_of = tables()
    slots = slots.reshape(64, 4) @ (1 << 2 * np.arange(4))
    f, y, core, zl, x = (lax.axis_index(name) for name in AXES)
    n = wavefield.shape[3]
    half = n // 2
    scale = 1.0 / jnp.sqrt(jnp.float32(wavefield.shape[2] * 16))
    quarter_code = looked_up([sum(q << 2 * i for i, q in enumerate(QUARTERS[i // 4][i % 4])) for i in range(8)], f * 4 + y)

    def quarter_at(place):
        return (quarter_code >> (2 * place).astype(jnp.uint32)).astype(jnp.int32) & 3

    e_quarter, h_col = quarter_at(x) // 2, quarter_at(x) % 2
    e_col = e_quarter ^ core

    other = lax.dynamic_index_in_dim(wavefield, 1 - f, 0, keepdims=False)
    own = lax.dynamic_index_in_dim(first_of(wavefield, other), f, 0, keepdims=False)
    other = lax.ppermute(other, "zh", ring(2, 1))

    pieces0, pieces1 = gather_x(own), gather_x(other)
    block0, block1 = jnp.concatenate(pieces0, 1), jnp.concatenate(pieces1, 1)
    near, far = ([lax.ppermute(block, "y", ring(4, -step)) for block in (own, other)] for step in (1, 2))
    near[1], far[1] = lax.optimization_barrier((near[1], far[1], *pieces1[3:]))[:2]

    def half_of(block, h):
        return jnp.where(h == 0, block[..., :half], block[..., half:])

    def quarter(pair, number):
        return half_of(jnp.where(number // 2 == core, pair[0], pair[1]), number % 2)

    def quarters(place):
        return jnp.stack([quarter(near, quarter_at(place)), quarter(far, quarter_at(place))])

    def from_core(piece):
        return lax.ppermute(piece, "core", ring(2, 1))

    moved = [lax.ppermute(quarters((x + step) % 4), "x", ring(4, step)) for step in (-1, 1, 2)]
    mine = jnp.concatenate([quarters(x), *moved], axis=2)
    theirs = from_core(mine)
    mine0 = half_of(jnp.where(e_col == 0, block0, block1), h_col)
    theirs0 = from_core(mine0)

    rows = jnp.concatenate([block0, block1], axis=2)
    upper = lax.broadcasted_iota(jnp.int32, (n, n), 0) <= lax.broadcasted_iota(jnp.int32, (n, n), 1)
    upper_half = half_of(upper, h_col)
    cross = product(jnp.where(e_quarter == 1, block0, block1), theirs0)
    inner0 = product(rows, half_of(block0, h_col))
    inner1 = product(rows, half_of(block1, h_col))
    is0 = f == 0
    diag0, diag1 = jnp.where(is0, inner0[:, :n], inner1[:, n:]), jnp.where(is0, inner1[:, n:], inner0[:, :n])
    packed = jnp.stack([jnp.where(upper_half, d[0], d[1]) for d in (diag0, diag1)])
    inner = jnp.where(e_col == f, jnp.where(is0, inner0[:, n:], inner1[:, :n]), packed)

    rows2 = jnp.where(e_col == y // 2, block0, block1)
    order = looked_up(slots, ((f * 4 + y) * 2 + core) * 4 + x)
    arrived = []
    got = []
    for j in range(2):
        ours = (j ^ h_col) == core
        product1 = product(rows, jnp.where(ours, mine[0], theirs[0]))
        product2 = product(rows2, jnp.where(ours, mine[1], theirs[1]))
        blocks = jnp.stack([product1[:, :n], product1[:, n:], product2, jnp.where(ours, inner, cross)])
        if j == 1:
            blocks = first_of(blocks, *arrived)

        def partial_of(slot, blocks=blocks):
            return lax.dynamic_index_in_dim(blocks, (order >> (2 * slot).astype(jnp.uint32)).astype(jnp.int32) & 3, 0, keepdims=False)

        power = power_of(blocks)
        arrived = [lax.ppermute(packed_half(partial_of((zl + step) % 4), power), "zl", ring(4, step)) for step in (1, 2, 3)]
        held = (partial_of(zl) + sum(map(unpacked_half, arrived))) * scale
        if j == 1:
            held = first_of(held, *got[0])
        got.append([lax.ppermute(held, AXES, perms[2 * kind + j]) for kind in range(2)])

    row, col = rcv_of(f, y, core), zl * 4 + x
    case = looked_up(case_of @ (1 << 2 * np.arange(16, dtype=np.int64)), row) >> (2 * col).astype(jnp.uint32) & 3
    swapped = jnp.where(case == 0, row, col) % 2 == 1

    def joined(a, b):
        return jnp.where(swapped, jnp.concatenate([b, a], -1), jnp.concatenate([a, b], -1))

    first, second = (joined(got[0][kind], got[1][kind]) for kind in range(2))

    def unpack(packed):
        strict = lax.broadcasted_iota(jnp.int32, (n, n), 0) < lax.broadcasted_iota(jnp.int32, (n, n), 1)
        top, low = jnp.where(upper, packed, 0.0), jnp.where(upper, 0.0, packed)
        return jnp.stack([top + jnp.where(strict, packed, 0.0).T, low - low.T])

    def turned(block):
        return jnp.stack([block[0].T, -block[1].T])

    diag_first, diag_second = (unpack(jnp.where(is0, a[0], a[1])) for a in (first, second))
    out0 = jnp.where(case == 1, first, jnp.where(case == 0, turned(second), jnp.where(is0, diag_first, diag_second)))
    out1 = jnp.where(case == 1, second, jnp.where(case == 0, turned(first), jnp.where(is0, diag_second, diag_first)))
    return jnp.stack([out0, out1])


def solution(mesh):
    fine = Mesh(mesh.devices.reshape(SIZES), AXES)
    return jax.shard_map(
        body,
        mesh=fine,
        in_specs=(P(None, None, ("zl", "x"), ("zh", "y", "core")),),
        out_specs=P(None, None, ("zh", "y", "core"), ("zl", "x")),
        check_vma=False,
    )
```

```python
import jax
import jax.numpy as jnp
from jax import lax
from jax.sharding import Mesh
from jax.sharding import PartitionSpec as P

AXES = ("zh", "y", "core", "zl", "x")
SIZES = (2, 4, 2, 4, 4)


def ring(n, step):
    return [(i, (i + step) % n) for i in range(n)]


def gather_x(block):
    half = block.shape[1] // 2
    above = lax.ppermute(block, "x", ring(4, -1))
    below = lax.ppermute(block, "x", ring(4, 1))
    far_a = lax.ppermute(above[:, :half], "x", ring(4, -1))
    far_b = lax.ppermute(below[:, half:], "x", ring(4, 1))
    return [block, above, below, far_a, far_b]


def chosen(options, index):
    out = options[0]
    for i in range(1, len(options)):
        out = jnp.where(index == i, options[i], out)
    return out


def product(cols, rows):
    return jnp.einsum("psc,psm->cm", cols, rows, preferred_element_type=jnp.float32)


def power_of(*arrays):
    top = max_of(*arrays)
    return jnp.clip(jnp.floor(jnp.log2(top)), -50.0, 50.0)


def max_of(*arrays):
    top = jnp.float32(0.0)
    for a in arrays:
        top = jnp.maximum(top, jnp.max(jnp.abs(a)).astype(jnp.float32))
    return top


def pattern(rows, cols):
    i = lax.broadcasted_iota(jnp.int32, (rows, cols), 0)
    j = lax.broadcasted_iota(jnp.int32, (rows, cols), 1)
    return ((i * 157 + j * 91) % 256 - 127.5).astype(jnp.float32) * 2.0**-18


def body(wavefield):
    f, y, core, zl, x = (lax.axis_index(name) for name in AXES)
    n = wavefield.shape[3]
    group = n // 4
    scale = 1.0 / jnp.sqrt(jnp.float32(wavefield.shape[2] * 16))
    is0 = f == 0

    other = lax.dynamic_index_in_dim(wavefield, 1 - f, 0, keepdims=False)
    own = lax.dynamic_index_in_dim(lax.optimization_barrier((wavefield, other))[0], f, 0, keepdims=False)
    other = lax.ppermute(other, "zh", ring(2, 1))

    pieces0, pieces1 = gather_x(own), gather_x(other)
    near = {step: [lax.ppermute(block, "y", ring(4, -step)) for block in (own, other)] for step in (1, 3)}

    def in_order(pair):
        return [jnp.where(is0, pair[0], pair[1]), jnp.where(is0, pair[1], pair[0])]

    def columns(pair, number):
        options = [
            jnp.concatenate([block[..., i * group : (i + 1) * group] for block in pair], -1) for i in range(4)
        ]
        return chosen(options, number)

    block0, block1 = in_order([jnp.concatenate(pieces0, 1), jnp.concatenate(pieces1, 1)])
    mine0 = columns([block0, block1], x)
    far = lax.ppermute(mine0, "y", ring(4, -2))
    near = {step: in_order(pair) for step, pair in near.items()}

    def near_columns(place):
        return jnp.concatenate([columns(near[1], place), columns(near[3], place)], -1)

    moved = [lax.ppermute(near_columns((x + step) % 4), "x", ring(4, step)) for step in (-1, 1, 2)]
    mine = jnp.concatenate([jnp.concatenate([near_columns(x), *moved], 1), far], -1)

    def from_core(piece):
        return lax.ppermute(piece, "core", ring(2, 1))

    theirs0, theirs = from_core(mine0), from_core(mine)

    rows = jnp.concatenate([block0, block1], -1)
    turned = jnp.stack([jnp.concatenate([rows[0], -rows[1]], -1), jnp.concatenate([rows[1], rows[0]], -1)])
    terms = []
    for zero, rest in ((mine0, mine), (theirs0, theirs)):
        one, three, two = jnp.split(product(rest, turned), 3, 0)
        terms.append([product(zero, turned), one, two, three])
    power = power_of(rows) + power_of(mine0, mine, theirs0, theirs)
    dither = pattern(group, n)
    factor = jnp.exp2(1.0 - power) * (1.0 + dither)

    table = jnp.stack([terms[k][d] for k in range(2) for d in range(4)])
    chunks = []
    for yc in range(4):
        for kc in range(2):
            which = (kc ^ core) * 4 + (yc - y) % 4
            piece = lax.dynamic_index_in_dim(table, which, 0, keepdims=False)
            chunks.append(piece.reshape(2, group, 2, 2, n).transpose(3, 0, 2, 1, 4))
    sent = jnp.stack(chunks, 2) * factor
    sent = sent.reshape(32, 2 * group, n).astype(jnp.float16)
    sent = jnp.concatenate([sent, jnp.full((32, 8, n), power, jnp.float16)], 1)
    got = lax.all_to_all(sent, ("zh", "zl", "x"), 0, 0, tiled=True)

    weight = jnp.exp2(got[:, -1, 0].astype(jnp.float32) - 1.0) * scale
    values = got[:, :-8].astype(jnp.float32) * weight[:, None, None]
    values = values.reshape(2, 4, 4, 2, group, n).sum(1) * (1.0 - dither)
    return values.transpose(0, 2, 4, 1, 3).reshape(2, 2, n, n)


def solution(mesh):
    fine = Mesh(mesh.devices.reshape(SIZES), AXES)
    return jax.shard_map(
        body,
        mesh=fine,
        in_specs=(P(None, None, ("zl", "x"), ("zh", "y", "core")),),
        out_specs=P(None, None, ("zh", "y", "core"), ("zl", "x")),
        check_vma=False,
    )
```

```python
import jax
import jax.numpy as jnp
from jax import lax
from jax.experimental import pallas as pl
from jax.experimental.pallas import tpu as pltpu
from jax.sharding import Mesh
from jax.sharding import PartitionSpec as P

AXES = ("zh", "y", "core", "zl", "x")
SIZES = (2, 4, 2, 4, 4)
TOP = 12


def ring(n, step):
    return [(i, (i + step) % n) for i in range(n)]


def first_of(value, *after):
    return lax.optimization_barrier((value, *after))[0]


def gather_x(block):
    half = block.shape[1] // 2
    above = lax.ppermute(block, "x", ring(4, -1))
    below = lax.ppermute(block, "x", ring(4, 1))
    far_a = lax.ppermute(above[:, :half], "x", ring(4, -1))
    far_b = lax.ppermute(below[:, half:], "x", ring(4, 1))
    return [block, above, below, far_a, far_b]


def terms_kernel(place, rows, zero, rest, out, top):
    f, y = place[0], place[1]
    n, c = out.shape[3:]
    first = lax.broadcasted_iota(jnp.int32, (n, 2 * c), 1) % c < c // 2
    top[...] = jnp.zeros_like(top)

    def one(cols, yc):
        weights = jnp.concatenate([cols[0], cols[1]], axis=1)
        for e in range(2):
            real = jnp.dot(rows[0, e], weights, preferred_element_type=jnp.float32)
            imag = jnp.dot(rows[1, e], weights, preferred_element_type=jnp.float32)
            turned = jnp.concatenate([pltpu.roll(imag[:, :c], c // 2, 1), pltpu.roll(imag[:, c:], c // 2, 1)], axis=1)
            term = real + jnp.where(first, turned, -turned)
            for g in range(2):
                out[f ^ e, f ^ g, yc] = term[:, g * c : (g + 1) * c]
            size = jnp.abs(term).reshape(n // 8, 8, 2 * c).max(0)
            top[...] = jnp.maximum(top[...], jnp.maximum(size[:, :c], size[:, c:]))

    one(zero, y)

    def step(d, carry):
        one(rest.at[d], lax.rem(y + d + 1, 4))
        return carry

    lax.fori_loop(0, 3, step, 0)


def terms_of(place, rows, zero, rest):
    n, shots = rows.shape[2:]
    c = zero.shape[2]
    return pl.pallas_call(
        terms_kernel,
        out_shape=(jax.ShapeDtypeStruct((2, 2, 4, n, c), jnp.float32), jax.ShapeDtypeStruct((8, c), jnp.float32)),
        in_specs=[pl.BlockSpec(memory_space=pltpu.SMEM)] + [pl.BlockSpec(memory_space=pltpu.VMEM)] * 3,
        out_specs=(pl.BlockSpec(memory_space=pltpu.VMEM),) * 2,
        compiler_params=pltpu.CompilerParams(vmem_limit_bytes=40 * 2**20),
        cost_estimate=pl.CostEstimate(flops=64 * n * shots * c, bytes_accessed=10 * 2**20, transcendentals=0),
    )(place, rows, zero, rest)


def pattern(rows, cols):
    i = lax.broadcasted_iota(jnp.int32, (rows, cols), 0)
    j = lax.broadcasted_iota(jnp.int32, (rows, cols), 1)
    return ((i * 157 + j * 91) % 256 - 127.5).astype(jnp.float32) * 2.0**-18


def body(wavefield):
    f, y, core, zl, x = (lax.axis_index(name) for name in AXES)
    n = wavefield.shape[3]
    group = n // 4
    scale = 1.0 / jnp.sqrt(jnp.float32(wavefield.shape[2] * 16))

    other = lax.dynamic_index_in_dim(wavefield, 1 - f, 0, keepdims=False)
    own = lax.dynamic_index_in_dim(first_of(wavefield, other), f, 0, keepdims=False)
    other = lax.ppermute(other, "zh", ring(2, 1))

    def from_y(block, step):
        return lax.ppermute(block, "y", ring(4, -step))

    pieces0 = gather_x(own)
    near0 = [from_y(own, 1), from_y(own, 3)]
    other = first_of(other, *near0, *pieces0[3:])
    pieces1 = gather_x(other)
    near1 = [from_y(other, 1), from_y(other, 3)]

    def columns(block, number):
        out = None
        for i in range(4):
            option = jnp.concatenate([block[p, :, i * group : (i + 1) * group] for p in range(2)], -1)
            out = option if out is None else jnp.where(number == i, option, out)
        return out

    mine0 = jnp.stack([jnp.concatenate([columns(piece, x) for piece in pieces]) for pieces in (pieces0, pieces1)])
    far = from_y(mine0, 2)

    def near_columns(place):
        return jnp.stack([jnp.stack([columns(near[i], place) for near in (near0, near1)]) for i in range(2)])

    moved = [lax.ppermute(near_columns((x + step) % 4), "x", ring(4, step)) for step in (-1, 1, 2)]
    nears = jnp.concatenate([near_columns(x), *moved], 2)
    mine = jnp.stack([nears[0], far, nears[1]])

    def from_core(piece):
        return lax.ppermute(piece, "core", ring(2, 1))

    theirs0, theirs = from_core(mine0), from_core(mine)

    rows = jnp.stack(
        [jnp.concatenate([piece.transpose(0, 2, 1) for piece in pieces], 2) for pieces in (pieces0, pieces1)], 1
    )
    place = jnp.stack([f, y])
    terms0, top0 = terms_of(place, rows, mine0, mine)
    terms1, top1 = terms_of(place, rows, theirs0, theirs)
    table = jnp.stack([jnp.where(core == 0, terms0, terms1), jnp.where(core == 0, terms1, terms0)], 3)
    power = jnp.clip(jnp.floor(jnp.log2(jnp.max(jnp.maximum(top0, top1)))), -100.0, 100.0)

    dither = pattern(n, 2 * group)
    sent = (table.reshape(32, n, 2 * group) * (jnp.exp2(TOP - power) * (1.0 + dither))).astype(jnp.float16)
    sent = jnp.concatenate([sent, jnp.full((32, 8, 2 * group), power, jnp.float16)], 1)
    got = lax.all_to_all(sent, ("zh", "zl", "x"), 0, 0, tiled=True)

    weight = jnp.exp2(got[:, -1, 0].astype(jnp.float32) - TOP) * scale
    values = got[:, :-8].astype(jnp.float32) * weight[:, None, None]
    values = values.reshape(2, 4, 4, n, 2 * group).sum(1) * (1.0 - dither)
    return jnp.stack(
        [
            jnp.concatenate([values[:, i, :, p * group : (p + 1) * group] for i in range(4)], -1)
            for p in range(2)
        ],
        1,
    )


def solution(mesh):
    fine = Mesh(mesh.devices.reshape(SIZES), AXES)
    return jax.shard_map(
        body,
        mesh=fine,
        in_specs=(P(None, None, ("zl", "x"), ("zh", "y", "core")),),
        out_specs=P(None, None, ("zh", "y", "core"), ("zl", "x")),
        check_vma=False,
    )
```

```python
import jax
import jax.numpy as jnp
from jax import lax
from jax.experimental import pallas as pl
from jax.experimental.pallas import tpu as pltpu
from jax.sharding import Mesh
from jax.sharding import PartitionSpec as P

AXES = ("zh", "y", "core", "zl", "x")
SIZES = (2, 4, 2, 4, 4)
TOP = 12


def ring(n, step):
    return [(i, (i + step) % n) for i in range(n)]


def first_of(value, *after):
    return lax.optimization_barrier((value, *after))[0]


def gather_x(block):
    half = block.shape[1] // 2
    above = lax.ppermute(block, "x", ring(4, -1))
    below = lax.ppermute(block, "x", ring(4, 1))
    far_a = lax.ppermute(above[:, :half], "x", ring(4, -1))
    far_b = lax.ppermute(below[:, half:], "x", ring(4, 1))
    return [block, above, below, far_a, far_b]


def add_terms(place, rows0, rows1, cols, out, top):
    f, y = place[0], place[1]
    n, c = out.shape[2:]
    first = lax.broadcasted_iota(jnp.int32, (n, 2 * c), 1) % c < c // 2
    top[...] = jnp.zeros_like(top)
    for dy in (0, 2):
        weights = jnp.concatenate([cols[dy], cols[dy + 1]], axis=1)
        for e, rows in enumerate((rows0, rows1)):
            real = jnp.dot(rows[0], weights, preferred_element_type=jnp.float32)
            imag = jnp.dot(rows[1], weights, preferred_element_type=jnp.float32)
            turned = jnp.concatenate([pltpu.roll(imag[:, :c], c // 2, 1), pltpu.roll(imag[:, c:], c // 2, 1)], axis=1)
            term = real + jnp.where(first, turned, -turned)
            for i in range(2):
                out[f ^ e, lax.rem(y + dy + i, 4)] = term[:, i * c : (i + 1) * c]
            size = jnp.abs(term).reshape(n // 8, 8, 2 * c).max(0)
            top[...] = jnp.maximum(top[...], jnp.maximum(size[:, :c], size[:, c:]))


def last_kernel(place, rows0, rows1, cols, term0, top0, term1, top1, term2, top2, out, term3, top3):
    add_terms(place, rows0, rows1, cols, term3, top3)
    f, core = place[0], place[2]
    n, c = term3.shape[2:]
    largest = jnp.max(jnp.maximum(jnp.maximum(top0[...], top1[...]), jnp.maximum(top2[...], top3[...])))
    power = jnp.clip(jnp.floor(jnp.log2(jnp.full((8, c), largest))), -100.0, 100.0)
    factor = jnp.exp2(TOP - power[:1]) * (1.0 + pattern(n, c))

    def step(i, carry):
        zr, yc = i // 4, lax.rem(i, 4)
        for number, term in enumerate((term0, term1, term2, term3)):
            zc, core_col = f ^ (number // 2), core ^ (number % 2)
            owner = zr * 16 + zc * 8 + yc * 2 + core_col
            out[owner, :n] = term[zr, yc] * factor
            out[owner, n:] = power
        return carry

    lax.fori_loop(0, 8, step, 0)


def terms_of(place, rows, cols, others=None):
    n, shots = rows[0].shape[1:]
    c = cols.shape[2]
    term = (2, 4, n, c)
    space = pl.BlockSpec(memory_space=pltpu.VMEM)
    if others is None:
        kernel, operands, scratch = add_terms, (place, *rows, cols), []
        shapes = (jax.ShapeDtypeStruct(term, jnp.float32), jax.ShapeDtypeStruct((8, c), jnp.float32))
    else:
        kernel, operands = last_kernel, (place, *rows, cols, *others)
        scratch = [pltpu.VMEM(term, jnp.float32), pltpu.VMEM((8, c), jnp.float32)]
        shapes = jax.ShapeDtypeStruct((32, n + 8, c), jnp.float32)
    return pl.pallas_call(
        kernel,
        out_shape=shapes,
        in_specs=[pl.BlockSpec(memory_space=pltpu.SMEM)] + [space] * (len(operands) - 1),
        out_specs=space if others else (space, space),
        scratch_shapes=scratch,
        compiler_params=pltpu.CompilerParams(vmem_limit_bytes=40 * 2**20),
        cost_estimate=pl.CostEstimate(flops=32 * n * shots * c, bytes_accessed=8 * 2**20, transcendentals=0),
    )(*operands)


def pattern(rows, cols):
    i = lax.broadcasted_iota(jnp.int32, (rows, cols), 0)
    j = lax.broadcasted_iota(jnp.int32, (rows, cols), 1)
    return ((i * 157 + j * 91) % 256 - 127.5).astype(jnp.float32) * 2.0**-18


def body(wavefield):
    f, y, core, zl, x = (lax.axis_index(name) for name in AXES)
    n = wavefield.shape[3]
    group = n // 4
    scale = 1.0 / jnp.sqrt(jnp.float32(wavefield.shape[2] * 16))

    other = lax.dynamic_index_in_dim(wavefield, 1 - f, 0, keepdims=False)
    own = lax.dynamic_index_in_dim(first_of(wavefield, other), f, 0, keepdims=False)
    other = lax.ppermute(other, "zh", ring(2, 1))

    def from_y(block, step):
        return lax.ppermute(block, "y", ring(4, -step))

    def from_core(piece):
        return lax.ppermute(piece, "core", ring(2, 1))

    def columns(block, number):
        out = None
        for i in range(4):
            option = jnp.concatenate([block[p, :, i * group : (i + 1) * group] for p in range(2)], -1)
            out = option if out is None else jnp.where(number == i, option, out)
        return out

    def gathered(block):
        pieces = gather_x(block)
        near = [from_y(block, 1), from_y(block, 3)]

        def near_columns(place):
            return jnp.stack([columns(piece, place) for piece in near])

        moved = [lax.ppermute(near_columns((x + step) % 4), "x", ring(4, step)) for step in (-1, 1, 2)]
        above, below = jnp.concatenate([near_columns(x), *moved], 1)
        here = jnp.concatenate([columns(piece, x) for piece in pieces])
        far = from_y(here, 2)
        rows = jnp.concatenate([piece.transpose(0, 2, 1) for piece in pieces], 2)
        return rows, jnp.stack([here, above, far, below]), [*pieces[3:], *near, *moved, far]

    rows0, mine0, done0 = gathered(own)
    rows1, mine1, _ = gathered(first_of(other, *done0))
    rows = (rows0, rows1)

    place = jnp.stack([f, y, core])
    ready = (*terms_of(place, rows, mine0), *terms_of(place, rows, from_core(mine0)))
    mine1, *ready = lax.optimization_barrier((mine1, *ready))
    theirs1 = from_core(mine1)
    ready = (*ready, *terms_of(place, rows, mine1))
    sent = terms_of(place, rows, theirs1, ready).astype(jnp.float16)
    got = lax.all_to_all(sent, ("zh", "zl", "x"), 0, 0, tiled=True)

    weight = jnp.exp2(got[:, n, 0].astype(jnp.float32) - TOP) * scale
    weight = weight.reshape(2, 4, 4, 1, 1)
    got = got[:, :n].reshape(2, 4, 4, n, 2 * group)
    values = sum(got[:, i].astype(jnp.float32) * weight[:, i] for i in range(4)) * (1.0 - pattern(n, 2 * group))
    return jnp.stack(
        [
            jnp.concatenate([values[:, i, :, p * group : (p + 1) * group] for i in range(4)], -1)
            for p in range(2)
        ],
        1,
    )


def solution(mesh):
    fine = Mesh(mesh.devices.reshape(SIZES), AXES)
    return jax.shard_map(
        body,
        mesh=fine,
        in_specs=(P(None, None, ("zl", "x"), ("zh", "y", "core")),),
        out_specs=P(None, None, ("zh", "y", "core"), ("zl", "x")),
        check_vma=False,
    )
```

```python
import jax
import jax.numpy as jnp
from jax import lax
from jax.experimental import pallas as pl
from jax.experimental.pallas import tpu as pltpu
from jax.sharding import Mesh
from jax.sharding import PartitionSpec as P

AXES = ("zh", "y", "core", "zl", "x")
SIZES = (2, 4, 2, 4, 4)
TOP = 12


def ring(n, step):
    return [(i, (i + step) % n) for i in range(n)]


def first_of(value, *after):
    return lax.optimization_barrier((value, *after))[0]


def gather_x(block):
    half = block.shape[1] // 2
    above = lax.ppermute(block, "x", ring(4, -1))
    below = lax.ppermute(block, "x", ring(4, 1))
    far_a = lax.ppermute(above[:, :half], "x", ring(4, -1))
    far_b = lax.ppermute(below[:, half:], "x", ring(4, 1))
    return [block, above, below, far_a, far_b]


def add_terms(place, *refs):
    f, y = place[0], place[1]
    blocks, (cols, out, top) = (refs[:5], refs[5:10]), refs[10:]
    n, c = out.shape[2:]
    first = lax.broadcasted_iota(jnp.int32, (n, 2 * c), 1) % c < c // 2
    top[...] = jnp.zeros_like(top)
    for dy in (0, 2):
        for e, pieces in enumerate(blocks):
            real = imag = 0.0
            start = 0
            for piece in pieces:
                here = slice(start, start + piece.shape[1])
                start = here.stop
                weights = jnp.concatenate([cols[dy, here], cols[dy + 1, here]], axis=1)
                real += across(piece[0], weights)
                imag += across(piece[1], weights)
            turned = jnp.concatenate([pltpu.roll(imag[:, :c], c // 2, 1), pltpu.roll(imag[:, c:], c // 2, 1)], axis=1)
            term = real + jnp.where(first, turned, -turned)
            for i in range(2):
                out[f ^ e, lax.rem(y + dy + i, 4)] = term[:, i * c : (i + 1) * c]
            size = jnp.abs(term).reshape(n // 8, 8, 2 * c).max(0)
            top[...] = jnp.maximum(top[...], jnp.maximum(size[:, :c], size[:, c:]))


def across(a, b):
    return lax.dot_general(a, b, (((0,), (0,)), ((), ())), preferred_element_type=jnp.float32)


def group_of(block, number):
    size = block.shape[2] // 4
    return jnp.concatenate([block[p, :, number * size : (number + 1) * size] for p in range(2)], axis=1)


def near_kernel(x, above, below, *outs):
    for place in range(4):

        @pl.when(x[0] == place)
        def _():
            for out, step in zip(outs, (0, -1, 1, 2)):
                for i, block in enumerate((above, below)):
                    out[i] = group_of(block, (place + step) % 4)


def own_kernel(x, *refs):
    out = refs[-1]
    for place in range(4):

        @pl.when(x[0] == place)
        def _():
            start = 0
            for piece in refs[:-1]:
                out[start : start + piece.shape[1]] = group_of(piece, place)
                start += piece.shape[1]


def join_kernel(here, far, *refs):
    out = refs[-1]
    out[0], out[2] = here[...], far[...]
    for i, ref in enumerate(refs[:-1]):
        s = ref.shape[1]
        out[1, i * s : (i + 1) * s], out[3, i * s : (i + 1) * s] = ref[0], ref[1]


SPACE = pl.BlockSpec(memory_space=pltpu.VMEM)
SCALAR = pl.BlockSpec(memory_space=pltpu.SMEM)
PARAMS = pltpu.CompilerParams(vmem_limit_bytes=40 * 2**20)


def small_call(kernel, shapes, *operands, scalars=1):
    size = sum(2 * a.size for a in operands[scalars:])
    return pl.pallas_call(
        kernel,
        out_shape=shapes,
        in_specs=[SCALAR] * scalars + [SPACE] * (len(operands) - scalars),
        out_specs=jax.tree.map(lambda _: SPACE, shapes),
        compiler_params=PARAMS,
        cost_estimate=pl.CostEstimate(flops=0, bytes_accessed=size, transcendentals=0),
    )(*operands)


def last_kernel(place, *refs):
    term0, top0, term1, top1, term2, top2, out, term3, top3 = refs[11:]
    add_terms(place, *refs[:11], term3, top3)
    f, core = place[0], place[2]
    n, c = term3.shape[2:]
    largest = jnp.max(jnp.maximum(jnp.maximum(top0[...], top1[...]), jnp.maximum(top2[...], top3[...])))
    power = jnp.clip(jnp.floor(jnp.log2(jnp.full((8, c), largest))), -100.0, 100.0)
    factor = jnp.exp2(TOP - power[:1]) * (1.0 + pattern(n, c))

    def step(i, carry):
        zr, yc = i // 4, lax.rem(i, 4)
        for number, term in enumerate((term0, term1, term2, term3)):
            zc, core_col = f ^ (number // 2), core ^ (number % 2)
            owner = zr * 16 + zc * 8 + yc * 2 + core_col
            out[owner, :n] = term[zr, yc] * factor
            out[owner, n:] = power
        return carry

    lax.fori_loop(0, 8, step, 0)


def terms_of(place, rows, cols, others=None):
    n, c = rows[0].shape[2], cols.shape[2]
    term = (2, 4, n, c)
    if others is None:
        kernel, operands, scratch = add_terms, (place, *rows, cols), []
        shapes = (jax.ShapeDtypeStruct(term, jnp.float32), jax.ShapeDtypeStruct((8, c), jnp.float32))
    else:
        kernel, operands = last_kernel, (place, *rows, cols, *others)
        scratch = [pltpu.VMEM(term, jnp.float32), pltpu.VMEM((8, c), jnp.float32)]
        shapes = jax.ShapeDtypeStruct((32, n + 8, c), jnp.float32)
    return pl.pallas_call(
        kernel,
        out_shape=shapes,
        in_specs=[SCALAR] + [SPACE] * (len(operands) - 1),
        out_specs=SPACE if others else (SPACE, SPACE),
        scratch_shapes=scratch,
        compiler_params=PARAMS,
        cost_estimate=pl.CostEstimate(flops=32 * n * cols.shape[1] * c, bytes_accessed=8 * 2**20, transcendentals=0),
    )(*operands)


def pattern(rows, cols):
    i = lax.broadcasted_iota(jnp.int32, (rows, cols), 0)
    j = lax.broadcasted_iota(jnp.int32, (rows, cols), 1)
    return ((i * 157 + j * 91) % 256 - 127.5).astype(jnp.float32) * 2.0**-18


def body(wavefield):
    f, y, core, zl, x = (lax.axis_index(name) for name in AXES)
    n = wavefield.shape[3]
    group = n // 4
    scale = 1.0 / jnp.sqrt(jnp.float32(wavefield.shape[2] * 16))

    other = lax.dynamic_index_in_dim(wavefield, 1 - f, 0, keepdims=False)
    own = lax.dynamic_index_in_dim(first_of(wavefield, other), f, 0, keepdims=False)
    other = lax.ppermute(other, "zh", ring(2, 1))

    def from_y(block, step):
        return lax.ppermute(block, "y", ring(4, -step))

    def from_core(piece):
        return lax.ppermute(piece, "core", ring(2, 1))

    def gathered(block):
        pieces = gather_x(block)
        near = [from_y(block, 1), from_y(block, 3)]
        cut = jax.ShapeDtypeStruct((2, block.shape[1], 2 * group), block.dtype)
        kept, *sent = small_call(near_kernel, (cut,) * 4, x[None], *near)
        moved = [lax.ppermute(part, "x", ring(4, step)) for part, step in zip(sent, (-1, 1, 2))]
        here = jax.ShapeDtypeStruct((4 * block.shape[1], 2 * group), block.dtype)
        here = small_call(own_kernel, here, x[None], *pieces)
        far = from_y(here, 2)
        cols = jax.ShapeDtypeStruct((4, *here.shape), block.dtype)
        cols = small_call(join_kernel, cols, here, far, kept, *moved, scalars=0)
        return pieces, cols, [*pieces[3:], *near]

    rows0, mine0, done0 = gathered(own)
    rows1, mine1, _ = gathered(first_of(other, *done0))
    rows = (*rows0, *rows1)

    place = jnp.stack([f, y, core])
    ready = (*terms_of(place, rows, mine0), *terms_of(place, rows, from_core(mine0)))
    mine1, *ready = lax.optimization_barrier((mine1, *ready))
    theirs1 = from_core(mine1)
    ready = (*ready, *terms_of(place, rows, mine1))
    sent = terms_of(place, rows, theirs1, ready).astype(jnp.float16)
    got = lax.all_to_all(sent, ("zh", "zl", "x"), 0, 0, tiled=True)

    weight = jnp.exp2(got[:, n, 0].astype(jnp.float32) - TOP) * scale
    weight = weight.reshape(2, 4, 4, 1, 1)
    got = got[:, :n].reshape(2, 4, 4, n, 2 * group)
    values = sum(got[:, i].astype(jnp.float32) * weight[:, i] for i in range(4)) * (1.0 - pattern(n, 2 * group))
    return jnp.stack(
        [
            jnp.concatenate([values[:, i, :, p * group : (p + 1) * group] for i in range(4)], -1)
            for p in range(2)
        ],
        1,
    )


def solution(mesh):
    fine = Mesh(mesh.devices.reshape(SIZES), AXES)
    return jax.shard_map(
        body,
        mesh=fine,
        in_specs=(P(None, None, ("zl", "x"), ("zh", "y", "core")),),
        out_specs=P(None, None, ("zh", "y", "core"), ("zl", "x")),
        check_vma=False,
    )
```

```python
import jax
import jax.numpy as jnp
from jax import lax
from jax.experimental import pallas as pl
from jax.experimental.pallas import tpu as pltpu
from jax.sharding import Mesh
from jax.sharding import PartitionSpec as P

AXES = ("zh", "y", "core", "zl", "x")
SIZES = (2, 4, 2, 4, 4)
TOP = 12


def ring(n, step):
    return [(i, (i + step) % n) for i in range(n)]


def first_of(value, *after):
    return lax.optimization_barrier((value, *after))[0]


def gather_x(block):
    half = block.shape[1] // 2
    above = lax.ppermute(block, "x", ring(4, -1))
    below = lax.ppermute(block, "x", ring(4, 1))
    far_a = lax.ppermute(above[:, :half], "x", ring(4, -1))
    far_b = lax.ppermute(below[:, half:], "x", ring(4, 1))
    return [block, above, below, far_a, far_b]


def add_terms(place, *refs):
    f, y = place[0], place[1]
    blocks, (cols, out, top) = (refs[:5], refs[5:10]), refs[10:]
    n, c = out.shape[2:]
    first = lax.broadcasted_iota(jnp.int32, (n, 2 * c), 1) % c < c // 2
    top[...] = jnp.zeros_like(top)
    for dy in (0, 2):
        for e, pieces in enumerate(blocks):
            real = imag = 0.0
            start = 0
            for piece in pieces:
                here = slice(start, start + piece.shape[1])
                start = here.stop
                weights = jnp.concatenate([cols[dy, here], cols[dy + 1, here]], axis=1)
                real += across(piece[0], weights)
                imag += across(piece[1], weights)
            turned = jnp.concatenate([pltpu.roll(imag[:, :c], c // 2, 1), pltpu.roll(imag[:, c:], c // 2, 1)], axis=1)
            term = real + jnp.where(first, turned, -turned)
            for i in range(2):
                out[f ^ e, lax.rem(y + dy + i, 4)] = term[:, i * c : (i + 1) * c]
            size = jnp.abs(term).reshape(n // 8, 8, 2 * c).max(0)
            top[...] = jnp.maximum(top[...], jnp.maximum(size[:, :c], size[:, c:]))


def across(a, b):
    return lax.dot_general(a, b, (((0,), (0,)), ((), ())), preferred_element_type=jnp.float32)


def group_of(block, number):
    size = block.shape[2] // 4
    return jnp.concatenate([block[p, :, number * size : (number + 1) * size] for p in range(2)], axis=1)


def near_kernel(x, above, below, *outs):
    for place in range(4):

        @pl.when(x[0] == place)
        def _():
            for out, step in zip(outs, (0, -1, 1, 2)):
                for i, block in enumerate((above, below)):
                    out[i] = group_of(block, (place + step) % 4)


def own_kernel(x, *refs):
    out = refs[-1]
    for place in range(4):

        @pl.when(x[0] == place)
        def _():
            start = 0
            for piece in refs[:-1]:
                out[start : start + piece.shape[1]] = group_of(piece, place)
                start += piece.shape[1]


def join_kernel(here, far, *refs):
    out = refs[-1]
    out[0], out[2] = here[...], far[...]
    for i, ref in enumerate(refs[:-1]):
        s = ref.shape[1]
        out[1, i * s : (i + 1) * s], out[3, i * s : (i + 1) * s] = ref[0], ref[1]


SPACE = pl.BlockSpec(memory_space=pltpu.VMEM)
SCALAR = pl.BlockSpec(memory_space=pltpu.SMEM)
PARAMS = pltpu.CompilerParams(vmem_limit_bytes=40 * 2**20)


def small_call(kernel, shapes, *operands, scalars=1):
    size = sum(2 * a.size for a in operands[scalars:])
    return pl.pallas_call(
        kernel,
        out_shape=shapes,
        in_specs=[SCALAR] * scalars + [SPACE] * (len(operands) - scalars),
        out_specs=jax.tree.map(lambda _: SPACE, shapes),
        compiler_params=PARAMS,
        cost_estimate=pl.CostEstimate(flops=0, bytes_accessed=size, transcendentals=0),
    )(*operands)


def last_kernel(place, *refs):
    term0, top0, term1, top1, term2, top2, out, term3, top3 = refs[11:]
    add_terms(place, *refs[:11], term3, top3)
    f, core = place[0], place[2]
    n, c = term3.shape[2:]
    largest = jnp.max(jnp.maximum(jnp.maximum(top0[...], top1[...]), jnp.maximum(top2[...], top3[...])))
    power = jnp.clip(jnp.floor(jnp.log2(jnp.full((8, c), largest))), -100.0, 100.0)
    factor = jnp.exp2(TOP - power[:1]) * (1.0 + pattern(n, c))

    def step(i, carry):
        zr, yc = i // 4, lax.rem(i, 4)
        for number, term in enumerate((term0, term1, term2, term3)):
            zc, core_col = f ^ (number // 2), core ^ (number % 2)
            owner = zr * 16 + zc * 8 + yc * 2 + core_col
            out[owner, :n] = term[zr, yc] * factor
            out[owner, n:] = power
        return carry

    lax.fori_loop(0, 8, step, 0)


def terms_of(place, rows, cols, others=None):
    n, c = rows[0].shape[2], cols.shape[2]
    term = (2, 4, n, c)
    if others is None:
        kernel, operands, scratch = add_terms, (place, *rows, cols), []
        shapes = (jax.ShapeDtypeStruct(term, jnp.float32), jax.ShapeDtypeStruct((8, c), jnp.float32))
    else:
        kernel, operands = last_kernel, (place, *rows, cols, *others)
        scratch = [pltpu.VMEM(term, jnp.float32), pltpu.VMEM((8, c), jnp.float32)]
        shapes = jax.ShapeDtypeStruct((32, n + 8, c), jnp.float32)
    return pl.pallas_call(
        kernel,
        out_shape=shapes,
        in_specs=[SCALAR] + [SPACE] * (len(operands) - 1),
        out_specs=SPACE if others else (SPACE, SPACE),
        scratch_shapes=scratch,
        compiler_params=PARAMS,
        cost_estimate=pl.CostEstimate(flops=32 * n * cols.shape[1] * c, bytes_accessed=8 * 2**20, transcendentals=0),
    )(*operands)


def pattern(rows, cols):
    i = lax.broadcasted_iota(jnp.int32, (rows, cols), 0)
    j = lax.broadcasted_iota(jnp.int32, (rows, cols), 1)
    return ((i * 157 + j * 91) % 256 - 127.5).astype(jnp.float32) * 2.0**-18


def body(wavefield):
    f, y, core, zl, x = (lax.axis_index(name) for name in AXES)
    n = wavefield.shape[3]
    group = n // 4
    scale = 1.0 / jnp.sqrt(jnp.float32(wavefield.shape[2] * 16))

    other = lax.dynamic_index_in_dim(wavefield, 1 - f, 0, keepdims=False)
    own = lax.dynamic_index_in_dim(first_of(wavefield, other), f, 0, keepdims=False)
    other = lax.ppermute(other, "zh", ring(2, 1))

    def from_y(block, step):
        return lax.ppermute(block, "y", ring(4, -step))

    def from_core(piece):
        return lax.ppermute(piece, "core", ring(2, 1))

    def gathered(block):
        pieces = gather_x(block)
        near = [from_y(block, 1), from_y(block, 3)]
        cut = jax.ShapeDtypeStruct((2, block.shape[1], 2 * group), block.dtype)
        kept, *sent = small_call(near_kernel, (cut,) * 4, x[None], *near)
        moved = [lax.ppermute(part, "x", ring(4, step)) for part, step in zip(sent, (-1, 1, 2))]
        here = jax.ShapeDtypeStruct((4 * block.shape[1], 2 * group), block.dtype)
        pieces[3:] = lax.optimization_barrier((*pieces[3:], kept))[:2]
        here = small_call(own_kernel, here, x[None], *pieces)
        far = from_y(here, 2)
        cols = jax.ShapeDtypeStruct((4, *here.shape), block.dtype)
        cols = small_call(join_kernel, cols, here, far, kept, *moved, scalars=0)
        return pieces, cols, [*pieces[3:], *near, *moved, far]

    rows0, mine0, done0 = gathered(own)
    rows1, mine1, _ = gathered(first_of(other, *done0))
    rows = (*rows0, *rows1)

    place = jnp.stack([f, y, core])
    theirs0 = from_core(mine0)
    mine1, *ready = lax.optimization_barrier((mine1, *terms_of(place, rows, mine0)))
    theirs1 = from_core(mine1)
    ready = (*ready, *terms_of(place, rows, theirs0), *terms_of(place, rows, mine1))
    sent = terms_of(place, rows, theirs1, ready).astype(jnp.float16)
    got = lax.all_to_all(sent, ("zh", "zl", "x"), 0, 0, tiled=True)

    weight = jnp.exp2(got[:, n, 0].astype(jnp.float32) - TOP) * scale
    weight = weight.reshape(2, 4, 4, 1, 1)
    got = got[:, :n].reshape(2, 4, 4, n, 2 * group)
    values = sum(got[:, i].astype(jnp.float32) * weight[:, i] for i in range(4)) * (1.0 - pattern(n, 2 * group))
    return jnp.stack(
        [
            jnp.concatenate([values[:, i, :, p * group : (p + 1) * group] for i in range(4)], -1)
            for p in range(2)
        ],
        1,
    )


def solution(mesh):
    fine = Mesh(mesh.devices.reshape(SIZES), AXES)
    return jax.shard_map(
        body,
        mesh=fine,
        in_specs=(P(None, None, ("zl", "x"), ("zh", "y", "core")),),
        out_specs=P(None, None, ("zh", "y", "core"), ("zl", "x")),
        check_vma=False,
    )
```

```python
import jax
import jax.numpy as jnp
from jax import lax
from jax.experimental import pallas as pl
from jax.experimental.pallas import tpu as pltpu
from jax.sharding import Mesh
from jax.sharding import PartitionSpec as P

AXES = ("zh", "y", "core", "zl", "x")
SIZES = (2, 4, 2, 4, 4)
TOP = 12


def ring(n, step):
    return [(i, (i + step) % n) for i in range(n)]


def first_of(value, *after):
    return lax.optimization_barrier((value, *after))[0]


def add_terms(place, *refs):
    f, y = place[0], place[1]
    blocks, (cols, out, top) = (refs[:5], refs[5:10]), refs[10:]
    n, c = out.shape[2:]
    first = lax.broadcasted_iota(jnp.int32, (n, 2 * c), 1) % c < c // 2
    top[...] = jnp.zeros_like(top)
    for dy in (0, 2):
        for e, pieces in enumerate(blocks):
            real = imag = 0.0
            start = 0
            for piece in pieces:
                here = slice(start, start + piece.shape[1])
                start = here.stop
                weights = jnp.concatenate([cols[dy, here], cols[dy + 1, here]], axis=1)
                real += across(piece[0], weights)
                imag += across(piece[1], weights)
            turned = jnp.concatenate([pltpu.roll(imag[:, :c], c // 2, 1), pltpu.roll(imag[:, c:], c // 2, 1)], axis=1)
            term = real + jnp.where(first, turned, -turned)
            for i in range(2):
                out[f ^ e, lax.rem(y + dy + i, 4)] = term[:, i * c : (i + 1) * c]
            size = jnp.abs(term).reshape(n // 8, 8, 2 * c).max(0)
            top[...] = jnp.maximum(top[...], jnp.maximum(size[:, :c], size[:, c:]))


def across(a, b):
    return lax.dot_general(a, b, (((0,), (0,)), ((), ())), preferred_element_type=jnp.float32)


def group_of(block, number):
    size = block.shape[2] // 4
    return jnp.concatenate([block[p, :, number * size : (number + 1) * size] for p in range(2)], axis=1)


def near_kernel(x, above, below, *outs):
    for place in range(4):

        @pl.when(x[0] == place)
        def _():
            for out, step in zip(outs, (0, -1, 1, 2)):
                for i, block in enumerate((above, below)):
                    out[i] = group_of(block, (place + step) % 4)


def own_kernel(x, *refs):
    out = refs[-1]
    for place in range(4):

        @pl.when(x[0] == place)
        def _():
            start = 0
            for piece in refs[:-1]:
                out[start : start + piece.shape[1]] = group_of(piece, place)
                start += piece.shape[1]


def join_kernel(here, far, *refs):
    *parts, out, done = refs
    copies = [(here, out.at[0]), (far, out.at[2])]
    for i, part in enumerate(parts):
        where = pl.ds(i * part.shape[1], part.shape[1])
        copies += [(part.at[0], out.at[1, where]), (part.at[1], out.at[3, where])]
    copies = [pltpu.make_async_copy(*ends, done.at[i]) for i, ends in enumerate(copies)]
    for copy in copies:
        copy.start()
    for copy in copies:
        copy.wait()


SPACE = pl.BlockSpec(memory_space=pltpu.VMEM)
SMALL, LARGE = 52 * 2**20, 52 * 2**20
SCALAR = pl.BlockSpec(memory_space=pltpu.SMEM)


def joined(shape, *parts):
    anywhere = pl.BlockSpec(memory_space=pl.ANY)
    return pl.pallas_call(
        join_kernel,
        out_shape=shape,
        in_specs=[anywhere] * len(parts),
        out_specs=anywhere,
        scratch_shapes=[pltpu.SemaphoreType.DMA((2 * len(parts) - 2,))],
        cost_estimate=pl.CostEstimate(flops=0, bytes_accessed=4 * sum(a.size for a in parts), transcendentals=0),
    )(*parts)


def small_call(kernel, shapes, *operands):
    size = sum(2 * a.size for a in operands[1:])
    return pl.pallas_call(
        kernel,
        out_shape=shapes,
        in_specs=[SCALAR] + [SPACE] * (len(operands) - 1),
        out_specs=jax.tree.map(lambda _: SPACE, shapes),
        compiler_params=pltpu.CompilerParams(vmem_limit_bytes=SMALL),
        cost_estimate=pl.CostEstimate(flops=0, bytes_accessed=size, transcendentals=0),
    )(*operands)


def last_kernel(place, *refs):
    term0, top0, term1, top1, term2, top2, out, term3, top3 = refs[11:]
    add_terms(place, *refs[:11], term3, top3)
    f, core = place[0], place[2]
    n, c = term3.shape[2:]
    largest = jnp.max(jnp.maximum(jnp.maximum(top0[...], top1[...]), jnp.maximum(top2[...], top3[...])))
    power = jnp.clip(jnp.floor(jnp.log2(jnp.full((16, c), largest))), -100.0, 100.0)
    factor = jnp.exp2(TOP - power[:1]) * (1.0 + pattern(n, c))

    def step(i, carry):
        zr, yc = i // 4, lax.rem(i, 4)
        for number, term in enumerate((term0, term1, term2, term3)):
            zc, core_col = f ^ (number // 2), core ^ (number % 2)
            owner = zr * 16 + zc * 8 + yc * 2 + core_col
            out[owner, :n] = term[zr, yc] * factor
            out[owner, n:] = power
        return carry

    lax.fori_loop(0, 8, step, 0)


def terms_of(place, rows, cols, others=None):
    n, c = rows[0].shape[2], cols.shape[2]
    term = (2, 4, n, c)
    if others is None:
        kernel, operands, scratch = add_terms, (place, *rows, cols), []
        shapes = (jax.ShapeDtypeStruct(term, jnp.float32), jax.ShapeDtypeStruct((8, c), jnp.float32))
    else:
        kernel, operands = last_kernel, (place, *rows, cols, *others)
        scratch = [pltpu.VMEM(term, jnp.float32), pltpu.VMEM((8, c), jnp.float32)]
        shapes = jax.ShapeDtypeStruct((32, n + 16, c), jnp.float32)
    return pl.pallas_call(
        kernel,
        out_shape=shapes,
        in_specs=[SCALAR] + [SPACE] * (len(operands) - 1),
        out_specs=SPACE if others else (SPACE, SPACE),
        scratch_shapes=scratch,
        compiler_params=pltpu.CompilerParams(vmem_limit_bytes=LARGE),
        cost_estimate=pl.CostEstimate(flops=32 * n * cols.shape[1] * c, bytes_accessed=8 * 2**20, transcendentals=0),
    )(*operands)


def pattern(rows, cols):
    i = lax.broadcasted_iota(jnp.int32, (rows, cols), 0)
    j = lax.broadcasted_iota(jnp.int32, (rows, cols), 1)
    return ((i * 157 + j * 91) % 256 - 127.5).astype(jnp.float32) * 2.0**-18


def body(wavefield):
    f, y, core, zl, x = (lax.axis_index(name) for name in AXES)
    n = wavefield.shape[3]
    group = n // 4
    scale = 1.0 / jnp.sqrt(jnp.float32(wavefield.shape[2] * 16))

    other = lax.dynamic_index_in_dim(wavefield, 1 - f, 0, keepdims=False)
    own = lax.dynamic_index_in_dim(first_of(wavefield, other), f, 0, keepdims=False)
    other = lax.ppermute(other, "zh", ring(2, 1))

    def from_y(block, step):
        return lax.ppermute(block, "y", ring(4, -step))

    def from_core(piece):
        return lax.ppermute(piece, "core", ring(2, 1))

    def gathered(block, *late):
        shots = block.shape[1]
        above, below = (lax.ppermute(block, "x", ring(4, step)) for step in (-1, 1))
        near = [from_y(block, 1), from_y(block, 3)]
        near = lax.optimization_barrier((*near, above, below))[:2]
        cut = jax.ShapeDtypeStruct((2, shots, 2 * group), block.dtype)
        kept, *sent = small_call(near_kernel, (cut,) * 4, x[None], *near)
        moved = [lax.ppermute(part, "x", ring(4, step)) for part, step in zip(sent, (-1, 1, 2))]
        far_a = lax.ppermute(above[:, : shots // 2], "x", ring(4, -1))
        far_b = lax.ppermute(below[:, shots // 2 :], "x", ring(4, 1))
        far_a, far_b = lax.optimization_barrier((far_a, far_b, kept, *late))[:2]
        pieces = [block, above, below, far_a, far_b]
        here = jax.ShapeDtypeStruct((4 * shots, 2 * group), block.dtype)
        here = small_call(own_kernel, here, x[None], *pieces)
        far = from_y(here, 2)
        cols = jax.ShapeDtypeStruct((4, *here.shape), block.dtype)
        cols = joined(cols, here, far, kept, *moved)
        return pieces, cols, moved

    rows0, mine0, moved0 = gathered(own, other)
    rows1, mine1, _ = gathered(first_of(other, *moved0))
    rows = (*rows0, *rows1)

    place = jnp.stack([f, y, core])
    theirs0 = from_core(mine0)
    mine1, *ready = lax.optimization_barrier((mine1, *terms_of(place, rows, mine0)))
    theirs1 = from_core(mine1)
    ready = (*ready, *terms_of(place, rows, theirs0), *terms_of(place, rows, mine1))
    sent = terms_of(place, rows, theirs1, ready).astype(jnp.float16)
    got = lax.all_to_all(sent, ("zh", "zl", "x"), 0, 0, tiled=True)

    weight = jnp.exp2(got[:, n, 0].astype(jnp.float32) - TOP) * scale
    undo = 1.0 - pattern(n, 2 * group)

    def owned(frequency, place):
        picked = [frequency * 16 + i * 4 + place for i in range(4)]
        return sum(got[i, :n].astype(jnp.float32) * weight[i] for i in picked) * undo

    values = [[owned(frequency, place) for place in range(4)] for frequency in range(2)]
    parts = [slice(p * group, (p + 1) * group) for p in range(2)]
    return jnp.stack([jnp.stack([jnp.concatenate([v[:, part] for v in row], -1) for part in parts]) for row in values])


def solution(mesh):
    fine = Mesh(mesh.devices.reshape(SIZES), AXES)
    return jax.shard_map(
        body,
        mesh=fine,
        in_specs=(P(None, None, ("zl", "x"), ("zh", "y", "core")),),
        out_specs=P(None, None, ("zh", "y", "core"), ("zl", "x")),
        check_vma=False,
    )
```

```python
import jax
import jax.numpy as jnp
from jax import lax
from jax.experimental import pallas as pl
from jax.experimental.pallas import tpu as pltpu
from jax.sharding import Mesh
from jax.sharding import PartitionSpec as P

AXES = ("zh", "y", "core", "zl", "x")
SIZES = (2, 4, 2, 4, 4)
TOP = 12


def ring(n, step):
    return [(i, (i + step) % n) for i in range(n)]


def first_of(value, *after):
    return lax.optimization_barrier((value, *after))[0]


def add_terms(place, *refs):
    f, y = place[0], place[1]
    blocks, (cols, out, top) = (refs[:5], refs[5:10]), refs[10:]
    n, c = out.shape[2:]
    first = lax.broadcasted_iota(jnp.int32, (n, 2 * c), 1) % c < c // 2
    top[...] = jnp.zeros_like(top)
    for dy in (0, 2):
        for e, pieces in enumerate(blocks):
            real = imag = 0.0
            start = 0
            for piece in pieces:
                here = slice(start, start + piece.shape[1])
                start = here.stop
                weights = jnp.concatenate([cols[dy, here], cols[dy + 1, here]], axis=1)
                real += across(piece[0], weights)
                imag += across(piece[1], weights)
            turned = jnp.concatenate([pltpu.roll(imag[:, :c], c // 2, 1), pltpu.roll(imag[:, c:], c // 2, 1)], axis=1)
            term = real + jnp.where(first, turned, -turned)
            for i in range(2):
                out[f ^ e, lax.rem(y + dy + i, 4)] = term[:, i * c : (i + 1) * c]
            size = jnp.abs(term).reshape(n // 8, 8, 2 * c).max(0)
            top[...] = jnp.maximum(top[...], jnp.maximum(size[:, :c], size[:, c:]))


def across(a, b):
    return lax.dot_general(a, b, (((0,), (0,)), ((), ())), preferred_element_type=jnp.float32)


def group_of(block, number):
    size = block.shape[2] // 4
    return jnp.concatenate([block[p, :, number * size : (number + 1) * size] for p in range(2)], axis=1)


def near_kernel(x, above, below, *outs):
    for place in range(4):

        @pl.when(x[0] == place)
        def _():
            for out, step in zip(outs, (0, -1, 1, 2)):
                for i, block in enumerate((above, below)):
                    out[i] = group_of(block, (place + step) % 4)


def own_kernel(x, *refs):
    out = refs[-1]
    for place in range(4):

        @pl.when(x[0] == place)
        def _():
            start = 0
            for piece in refs[:-1]:
                out[start : start + piece.shape[1]] = group_of(piece, place)
                start += piece.shape[1]


def join_kernel(here, far, *refs):
    out = refs[-1]
    out[0], out[2] = here[...], far[...]
    for i, ref in enumerate(refs[:-1]):
        s = ref.shape[1]
        out[1, i * s : (i + 1) * s], out[3, i * s : (i + 1) * s] = ref[0], ref[1]


SPACE = pl.BlockSpec(memory_space=pltpu.VMEM)
GRANT = 40 * 2**20
SCALAR = pl.BlockSpec(memory_space=pltpu.SMEM)


def small_call(kernel, shapes, *operands, scalars=1):
    size = sum(2 * a.size for a in operands[scalars:])
    return pl.pallas_call(
        kernel,
        out_shape=shapes,
        in_specs=[SCALAR] * scalars + [SPACE] * (len(operands) - scalars),
        out_specs=jax.tree.map(lambda _: SPACE, shapes),
        compiler_params=pltpu.CompilerParams(vmem_limit_bytes=GRANT),
        cost_estimate=pl.CostEstimate(flops=0, bytes_accessed=size, transcendentals=0),
    )(*operands)


def last_kernel(place, *refs):
    term0, top0, term1, top1, term2, top2, out, term3, top3 = refs[11:]
    add_terms(place, *refs[:11], term3, top3)
    f, core = place[0], place[2]
    n, c = term3.shape[2:]
    largest = jnp.max(jnp.maximum(jnp.maximum(top0[...], top1[...]), jnp.maximum(top2[...], top3[...])))
    power = jnp.clip(jnp.floor(jnp.log2(jnp.full((16, c), largest))), -100.0, 100.0)
    factor = jnp.exp2(TOP - power[:1]) * (1.0 + pattern(n, c))

    def step(i, carry):
        zr, yc = i // 4, lax.rem(i, 4)
        for number, term in enumerate((term0, term1, term2, term3)):
            zc, core_col = f ^ (number // 2), core ^ (number % 2)
            owner = zr * 16 + zc * 8 + yc * 2 + core_col
            out[owner, :n] = term[zr, yc] * factor
            out[owner, n:] = power
        return carry

    lax.fori_loop(0, 8, step, 0)


def terms_of(place, rows, cols, others=None):
    n, c = rows[0].shape[2], cols.shape[2]
    term = (2, 4, n, c)
    if others is None:
        kernel, operands, scratch = add_terms, (place, *rows, cols), []
        shapes = (jax.ShapeDtypeStruct(term, jnp.float32), jax.ShapeDtypeStruct((8, c), jnp.float32))
    else:
        kernel, operands = last_kernel, (place, *rows, cols, *others)
        scratch = [pltpu.VMEM(term, jnp.float32), pltpu.VMEM((8, c), jnp.float32)]
        shapes = jax.ShapeDtypeStruct((32, n + 16, c), jnp.float32)
    return pl.pallas_call(
        kernel,
        out_shape=shapes,
        in_specs=[SCALAR] + [SPACE] * (len(operands) - 1),
        out_specs=SPACE if others else (SPACE, SPACE),
        scratch_shapes=scratch,
        compiler_params=pltpu.CompilerParams(vmem_limit_bytes=GRANT),
        cost_estimate=pl.CostEstimate(flops=32 * n * cols.shape[1] * c, bytes_accessed=8 * 2**20, transcendentals=0),
    )(*operands)


def pattern(rows, cols):
    i = lax.broadcasted_iota(jnp.int32, (rows, cols), 0)
    j = lax.broadcasted_iota(jnp.int32, (rows, cols), 1)
    return ((i * 157 + j * 91) % 256 - 127.5).astype(jnp.float32) * 2.0**-18


def body(wavefield):
    f, y, core, zl, x = (lax.axis_index(name) for name in AXES)
    n = wavefield.shape[3]
    group = n // 4
    scale = 1.0 / jnp.sqrt(jnp.float32(wavefield.shape[2] * 16))

    other = lax.dynamic_index_in_dim(wavefield, 1 - f, 0, keepdims=False)
    own = lax.dynamic_index_in_dim(first_of(wavefield, other), f, 0, keepdims=False)
    other = lax.ppermute(other, "zh", ring(2, 1))

    def from_y(block, step):
        return lax.ppermute(block, "y", ring(4, -step))

    def from_core(piece):
        return lax.ppermute(piece, "core", ring(2, 1))

    def gathered(block, *late):
        shots = block.shape[1]
        above, below = (lax.ppermute(block, "x", ring(4, step)) for step in (-1, 1))
        near = [from_y(block, 1), from_y(block, 3)]
        near = lax.optimization_barrier((*near, above, below))[:2]
        cut = jax.ShapeDtypeStruct((2, shots, 2 * group), block.dtype)
        kept, *sent = small_call(near_kernel, (cut,) * 4, x[None], *near)
        moved = [lax.ppermute(part, "x", ring(4, step)) for part, step in zip(sent, (-1, 1, 2))]
        far_a = lax.ppermute(above[:, : shots // 2], "x", ring(4, -1))
        far_b = lax.ppermute(below[:, shots // 2 :], "x", ring(4, 1))
        far_a, far_b = lax.optimization_barrier((far_a, far_b, kept, *late))[:2]
        pieces = [block, above, below, far_a, far_b]
        here = jax.ShapeDtypeStruct((4 * shots, 2 * group), block.dtype)
        here = small_call(own_kernel, here, x[None], *pieces)
        far = from_y(here, 2)
        cols = jax.ShapeDtypeStruct((4, *here.shape), block.dtype)
        cols = small_call(join_kernel, cols, here, far, kept, *moved, scalars=0)
        return pieces, cols, moved

    rows0, mine0, moved0 = gathered(own, other)
    rows1, mine1, _ = gathered(first_of(other, *moved0))
    rows = (*rows0, *rows1)

    place = jnp.stack([f, y, core])
    theirs0 = from_core(mine0)
    mine1, *ready = lax.optimization_barrier((mine1, *terms_of(place, rows, mine0)))
    theirs1 = from_core(mine1)
    ready = (*ready, *terms_of(place, rows, theirs0), *terms_of(place, rows, mine1))
    sent = terms_of(place, rows, theirs1, ready).astype(jnp.float16)
    got = lax.all_to_all(sent, ("zh", "zl", "x"), 0, 0, tiled=True)

    got = got.reshape(2, 4, 4, n + 16, 2 * group)
    weight = jnp.exp2(got[..., n:, :].astype(jnp.float32)[..., :1, :1] - TOP) * scale
    values = sum(got[:, i, :, :n].astype(jnp.float32) * weight[:, i] for i in range(4)) * (1.0 - pattern(n, 2 * group))
    return jnp.stack(
        [
            jnp.concatenate([values[:, i, :, p * group : (p + 1) * group] for i in range(4)], -1)
            for p in range(2)
        ],
        1,
    )


def solution(mesh):
    fine = Mesh(mesh.devices.reshape(SIZES), AXES)
    return jax.shard_map(
        body,
        mesh=fine,
        in_specs=(P(None, None, ("zl", "x"), ("zh", "y", "core")),),
        out_specs=P(None, None, ("zh", "y", "core"), ("zl", "x")),
        check_vma=False,
    )
```

```python
import functools

import jax
import jax.numpy as jnp
from jax import lax
from jax.experimental import pallas as pl
from jax.experimental.pallas import tpu as pltpu
from jax.sharding import Mesh
from jax.sharding import PartitionSpec as P

AXES = ("zh", "y", "core", "zl", "x")
SIZES = (2, 4, 2, 4, 4)
TOP = 12


def ring(n, step):
    return [(i, (i + step) % n) for i in range(n)]


def first_of(value, *after):
    return lax.optimization_barrier((value, *after))[0]


def add_terms(place, *refs):
    f, y = place[0], place[1]
    blocks, (cols, out, top) = (refs[:5], refs[5:10]), refs[10:]
    n, c = out.shape[2:]
    first = lax.broadcasted_iota(jnp.int32, (n, 2 * c), 1) % c < c // 2
    top[...] = jnp.zeros_like(top)
    for dy in (0, 2):
        for e, pieces in enumerate(blocks):
            real = imag = 0.0
            start = 0
            for piece in pieces:
                here = slice(start, start + piece.shape[1])
                start = here.stop
                weights = jnp.concatenate([cols[dy, here], cols[dy + 1, here]], axis=1)
                real += across(piece[0], weights)
                imag += across(piece[1], weights)
            turned = jnp.concatenate([pltpu.roll(imag[:, :c], c // 2, 1), pltpu.roll(imag[:, c:], c // 2, 1)], axis=1)
            term = real + jnp.where(first, turned, -turned)
            for i in range(2):
                out[f ^ e, lax.rem(y + dy + i, 4)] = term[:, i * c : (i + 1) * c]
            size = jnp.abs(term).reshape(n // 8, 8, 2 * c).max(0)
            top[...] = jnp.maximum(top[...], jnp.maximum(size[:, :c], size[:, c:]))


def across(a, b):
    return lax.dot_general(a, b, (((0,), (0,)), ((), ())), preferred_element_type=jnp.float32)


def group_of(block, number):
    size = block.shape[2] // 4
    return jnp.concatenate([block[p, :, number * size : (number + 1) * size] for p in range(2)], axis=1)


def near_kernel(x, above, below, *outs):
    for place in range(4):

        @pl.when(x[0] == place)
        def _():
            for out, step in zip(outs, (0, -1, 1, 2)):
                for i, block in enumerate((above, below)):
                    out[i] = group_of(block, (place + step) % 4)


def own_kernel(x, *refs):
    out = refs[-1]
    for place in range(4):

        @pl.when(x[0] == place)
        def _():
            start = 0
            for piece in refs[:-1]:
                out[start : start + piece.shape[1]] = group_of(piece, place)
                start += piece.shape[1]


def join_kernel(here, far, *refs):
    out = refs[-1]
    out[0], out[2] = here[...], far[...]
    for i, ref in enumerate(refs[:-1]):
        s = ref.shape[1]
        out[1, i * s : (i + 1) * s], out[3, i * s : (i + 1) * s] = ref[0], ref[1]


SPACE = pl.BlockSpec(memory_space=pltpu.VMEM)
GRANT = 40 * 2**20
SCALAR = pl.BlockSpec(memory_space=pltpu.SMEM)


def small_call(kernel, shapes, *operands, scalars=1):
    size = sum(2 * a.size for a in operands[scalars:])
    return pl.pallas_call(
        kernel,
        out_shape=shapes,
        in_specs=[SCALAR] * scalars + [SPACE] * (len(operands) - scalars),
        out_specs=jax.tree.map(lambda _: SPACE, shapes),
        compiler_params=pltpu.CompilerParams(vmem_limit_bytes=GRANT),
        cost_estimate=pl.CostEstimate(flops=0, bytes_accessed=size, transcendentals=0),
    )(*operands)


def last_kernel(place, *refs):
    term0, top0, term1, top1, term2, top2, out, term3, top3 = refs[11:]
    add_terms(place, *refs[:11], term3, top3)
    f, core = place[0], place[2]
    n, c = term3.shape[2:]
    largest = jnp.max(jnp.maximum(jnp.maximum(top0[...], top1[...]), jnp.maximum(top2[...], top3[...])))
    power = jnp.clip(jnp.floor(jnp.log2(jnp.full((8, c), largest))), -100.0, 100.0)
    factor = jnp.exp2(TOP - power[:1]) * (1.0 + pattern(n, c))

    def step(i, carry):
        zr, yc = i // 4, lax.rem(i, 4)
        for number, term in enumerate((term0, term1, term2, term3)):
            zc, core_col = f ^ (number // 2), core ^ (number % 2)
            owner = zr * 16 + zc * 8 + yc * 2 + core_col
            out[owner, :n] = term[zr, yc] * factor
            out[owner, n:] = power
        return carry

    lax.fori_loop(0, 8, step, 0)


def terms_of(place, rows, cols, others=None):
    n, c = rows[0].shape[2], cols.shape[2]
    term = (2, 4, n, c)
    if others is None:
        kernel, operands, scratch = add_terms, (place, *rows, cols), []
        shapes = (jax.ShapeDtypeStruct(term, jnp.float32), jax.ShapeDtypeStruct((8, c), jnp.float32))
    else:
        kernel, operands = last_kernel, (place, *rows, cols, *others)
        scratch = [pltpu.VMEM(term, jnp.float32), pltpu.VMEM((8, c), jnp.float32)]
        shapes = jax.ShapeDtypeStruct((32, n + 8, c), jnp.float32)
    return pl.pallas_call(
        kernel,
        out_shape=shapes,
        in_specs=[SCALAR] + [SPACE] * (len(operands) - 1),
        out_specs=SPACE if others else (SPACE, SPACE),
        scratch_shapes=scratch,
        compiler_params=pltpu.CompilerParams(vmem_limit_bytes=GRANT),
        cost_estimate=pl.CostEstimate(flops=32 * n * cols.shape[1] * c, bytes_accessed=8 * 2**20, transcendentals=0),
    )(*operands)


def sum_kernel(scale, got, out):
    n = out.shape[2]
    c = got.shape[2]
    undo = (1.0 - pattern(n, c)) * scale
    for f in range(2):
        for x in range(4):
            total = 0.0
            for zl in range(4):
                chunk = f * 16 + zl * 4 + x
                total += got[chunk, :n] * jnp.exp2(got[chunk, n : n + 1] - TOP)
            total *= undo
            for p in range(2):
                out[f, p, :, x * c // 2 : (x + 1) * c // 2] = total[:, p * c // 2 : (p + 1) * c // 2]


def pattern(rows, cols):
    i = lax.broadcasted_iota(jnp.int32, (rows, cols), 0)
    j = lax.broadcasted_iota(jnp.int32, (rows, cols), 1)
    return ((i * 157 + j * 91) % 256 - 127.5).astype(jnp.float32) * 2.0**-18


def body(wavefield):
    f, y, core, zl, x = (lax.axis_index(name) for name in AXES)
    n = wavefield.shape[3]
    group = n // 4

    other = lax.dynamic_index_in_dim(wavefield, 1 - f, 0, keepdims=False)
    own = lax.dynamic_index_in_dim(first_of(wavefield, other), f, 0, keepdims=False)
    other = lax.ppermute(other, "zh", ring(2, 1))

    def from_y(block, step):
        return lax.ppermute(block, "y", ring(4, -step))

    def from_core(piece):
        return lax.ppermute(piece, "core", ring(2, 1))

    def gathered(block, *late):
        shots = block.shape[1]
        above, below = (lax.ppermute(block, "x", ring(4, step)) for step in (-1, 1))
        near = [from_y(block, 1), from_y(block, 3)]
        near = lax.optimization_barrier((*near, above, below))[:2]
        cut = jax.ShapeDtypeStruct((2, shots, 2 * group), block.dtype)
        kept, *sent = small_call(near_kernel, (cut,) * 4, x[None], *near)
        moved = [lax.ppermute(part, "x", ring(4, step)) for part, step in zip(sent, (-1, 1, 2))]
        far_a = lax.ppermute(above[:, : shots // 2], "x", ring(4, -1))
        far_b = lax.ppermute(below[:, shots // 2 :], "x", ring(4, 1))
        far_a, far_b = lax.optimization_barrier((far_a, far_b, kept, *late))[:2]
        pieces = [block, above, below, far_a, far_b]
        here = jax.ShapeDtypeStruct((4 * shots, 2 * group), block.dtype)
        here = small_call(own_kernel, here, x[None], *pieces)
        far = from_y(here, 2)
        cols = jax.ShapeDtypeStruct((4, *here.shape), block.dtype)
        cols = small_call(join_kernel, cols, here, far, kept, *moved, scalars=0)
        return pieces, cols, moved

    rows0, mine0, moved0 = gathered(own, other)
    rows1, mine1, _ = gathered(first_of(other, *moved0))
    rows = (*rows0, *rows1)

    place = jnp.stack([f, y, core])
    theirs0 = from_core(mine0)
    mine1, *ready = lax.optimization_barrier((mine1, *terms_of(place, rows, mine0)))
    theirs1 = from_core(mine1)
    ready = (*ready, *terms_of(place, rows, theirs0), *terms_of(place, rows, mine1))
    sent = terms_of(place, rows, theirs1, ready).astype(jnp.float16)
    got = lax.all_to_all(sent, ("zh", "zl", "x"), 0, 0, tiled=True)

    whole = jax.ShapeDtypeStruct((2, 2, n, n), jnp.float32)
    kernel = functools.partial(sum_kernel, (16 * wavefield.shape[2]) ** -0.5)
    return small_call(kernel, whole, got.astype(jnp.float32), scalars=0)


def solution(mesh):
    fine = Mesh(mesh.devices.reshape(SIZES), AXES)
    return jax.shard_map(
        body,
        mesh=fine,
        in_specs=(P(None, None, ("zl", "x"), ("zh", "y", "core")),),
        out_specs=P(None, None, ("zh", "y", "core"), ("zl", "x")),
        check_vma=False,
    )
```

```python
import functools

import jax
import jax.numpy as jnp
from jax import lax
from jax.experimental import pallas as pl
from jax.experimental.pallas import tpu as pltpu
from jax.sharding import Mesh
from jax.sharding import PartitionSpec as P

AXES = ("zh", "y", "core", "zl", "x")
SIZES = (2, 4, 2, 4, 4)
TOP = 12


def ring(n, step):
    return [(i, (i + step) % n) for i in range(n)]


def first_of(value, *after):
    return lax.optimization_barrier((value, *after))[0]


def add_terms(place, *refs):
    f, y = place[0], place[1]
    blocks, (cols, out, top) = (refs[:4], refs[4:9]), refs[9:]
    n, c = out.shape[2:]
    first = lax.broadcasted_iota(jnp.int32, (n, 2 * c), 1) % c < c // 2
    top[...] = jnp.zeros_like(top)
    for dy in (0, 2):
        for e, pieces in enumerate(blocks):
            real = imag = 0.0
            start = 0
            for piece in pieces:
                here = slice(start, start + piece.shape[1])
                start = here.stop
                weights = jnp.concatenate([cols[dy, here], cols[dy + 1, here]], axis=1)
                real += across(piece[0], weights)
                imag += across(piece[1], weights)
            turned = jnp.concatenate([pltpu.roll(imag[:, :c], c // 2, 1), pltpu.roll(imag[:, c:], c // 2, 1)], axis=1)
            term = real + jnp.where(first, turned, -turned)
            for i in range(2):
                out[f ^ e, lax.rem(y + dy + i, 4)] = term[:, i * c : (i + 1) * c]
            size = jnp.abs(term).reshape(n // 8, 8, 2 * c).max(0)
            top[...] = jnp.maximum(top[...], jnp.maximum(size[:, :c], size[:, c:]))


def across(a, b):
    return lax.dot_general(a, b, (((0,), (0,)), ((), ())), preferred_element_type=jnp.float32)


def group_of(block, number):
    size = block.shape[2] // 4
    return jnp.concatenate([block[p, :, number * size : (number + 1) * size] for p in range(2)], axis=1)


def near_kernel(x, above, below, *outs):
    for place in range(4):

        @pl.when(x[0] == place)
        def _():
            for out, step in zip(outs, (0, -1, 1, 2)):
                for i, block in enumerate((above, below)):
                    out[i] = group_of(block, (place + step) % 4)


def own_kernel(x, *refs):
    out = refs[-1]
    for place in range(4):

        @pl.when(x[0] == place)
        def _():
            start = 0
            for piece in refs[:-1]:
                out[start : start + piece.shape[1]] = group_of(piece, place)
                start += piece.shape[1]


def join_kernel(here, far, *refs):
    out = refs[-1]
    out[0], out[2] = here[...], far[...]
    for i, ref in enumerate(refs[:-1]):
        s = ref.shape[1]
        out[1, i * s : (i + 1) * s], out[3, i * s : (i + 1) * s] = ref[0], ref[1]


SPACE = pl.BlockSpec(memory_space=pltpu.VMEM)
GRANT = 40 * 2**20
SCALAR = pl.BlockSpec(memory_space=pltpu.SMEM)


def small_call(kernel, shapes, *operands, scalars=1):
    size = sum(2 * a.size for a in operands[scalars:])
    return pl.pallas_call(
        kernel,
        out_shape=shapes,
        in_specs=[SCALAR] * scalars + [SPACE] * (len(operands) - scalars),
        out_specs=jax.tree.map(lambda _: SPACE, shapes),
        compiler_params=pltpu.CompilerParams(vmem_limit_bytes=GRANT),
        cost_estimate=pl.CostEstimate(flops=0, bytes_accessed=size, transcendentals=0),
    )(*operands)


def last_kernel(place, *refs):
    term0, top0, term1, top1, term2, top2, out, term3, top3 = refs[10:]
    add_terms(place, *refs[:10], term3, top3)
    f, core = place[0], place[2]
    n, c = term3.shape[2:]
    largest = jnp.max(jnp.maximum(jnp.maximum(top0[...], top1[...]), jnp.maximum(top2[...], top3[...])))
    power = jnp.clip(jnp.floor(jnp.log2(jnp.full((8, c), largest))), -100.0, 100.0)
    factor = jnp.exp2(TOP - power[:1]) * (1.0 + pattern(n, c))

    def step(i, carry):
        zr, yc = i // 4, lax.rem(i, 4)
        for number, term in enumerate((term0, term1, term2, term3)):
            zc, core_col = f ^ (number // 2), core ^ (number % 2)
            owner = zr * 16 + zc * 8 + yc * 2 + core_col
            out[owner, :n] = term[zr, yc] * factor
            out[owner, n:] = power
        return carry

    lax.fori_loop(0, 8, step, 0)


def terms_of(place, rows, cols, others=None):
    n, c = rows[0].shape[2], cols.shape[2]
    term = (2, 4, n, c)
    if others is None:
        kernel, operands, scratch = add_terms, (place, *rows, cols), []
        shapes = (jax.ShapeDtypeStruct(term, jnp.float32), jax.ShapeDtypeStruct((8, c), jnp.float32))
    else:
        kernel, operands = last_kernel, (place, *rows, cols, *others)
        scratch = [pltpu.VMEM(term, jnp.float32), pltpu.VMEM((8, c), jnp.float32)]
        shapes = jax.ShapeDtypeStruct((32, n + 8, c), jnp.float32)
    return pl.pallas_call(
        kernel,
        out_shape=shapes,
        in_specs=[SCALAR] + [SPACE] * (len(operands) - 1),
        out_specs=SPACE if others else (SPACE, SPACE),
        scratch_shapes=scratch,
        compiler_params=pltpu.CompilerParams(vmem_limit_bytes=GRANT),
        cost_estimate=pl.CostEstimate(flops=32 * n * cols.shape[1] * c, bytes_accessed=8 * 2**20, transcendentals=0),
    )(*operands)


def sum_kernel(scale, got, out):
    n = out.shape[2]
    c = got.shape[2]
    undo = (1.0 - pattern(n, c)) * scale
    for f in range(2):
        for x in range(4):
            total = 0.0
            for zl in range(4):
                chunk = f * 16 + zl * 4 + x
                total += got[chunk, :n] * jnp.exp2(got[chunk, n : n + 1] - TOP)
            total *= undo
            for p in range(2):
                out[f, p, :, x * c // 2 : (x + 1) * c // 2] = total[:, p * c // 2 : (p + 1) * c // 2]


def pattern(rows, cols):
    i = lax.broadcasted_iota(jnp.int32, (rows, cols), 0)
    j = lax.broadcasted_iota(jnp.int32, (rows, cols), 1)
    return ((i * 157 + j * 91) % 256 - 127.5).astype(jnp.float32) * 2.0**-18


def body(wavefield):
    f, y, core, zl, x = (lax.axis_index(name) for name in AXES)
    n = wavefield.shape[3]
    group = n // 4

    other = lax.dynamic_index_in_dim(wavefield, 1 - f, 0, keepdims=False)
    own = lax.dynamic_index_in_dim(first_of(wavefield, other), f, 0, keepdims=False)
    other = lax.ppermute(other, "zh", ring(2, 1))

    def from_y(block, step):
        return lax.ppermute(block, "y", ring(4, -step))

    def from_core(piece):
        return lax.ppermute(piece, "core", ring(2, 1))

    def gathered(block, ways, *late):
        shots = block.shape[1]
        above, below = (lax.ppermute(block, "x", ring(4, step)) for step in (-1, 1))
        near = [from_y(block, 1), from_y(block, 3)]
        near = lax.optimization_barrier((*near, above, below))[:2]
        cut = jax.ShapeDtypeStruct((2, shots, 2 * group), block.dtype)
        kept, *sent = small_call(near_kernel, (cut,) * 4, x[None], *near)
        moved = [lax.ppermute(part, "x", ring(4, step)) for part, step in zip(sent, (-1, 1, 2))]
        relayed = [lax.ppermute(above[:, : shots // ways], "x", ring(4, -1))]
        if ways == 2:
            relayed.append(lax.ppermute(below[:, shots // 2 :], "x", ring(4, 1)))
        done = [*moved, *relayed]
        pieces = [block, above, below, *lax.optimization_barrier((*relayed, kept, *late))[:ways]]
        here = jax.ShapeDtypeStruct((4 * shots, 2 * group), block.dtype)
        here = small_call(own_kernel, here, x[None], *pieces)
        far = from_y(here, 2)
        cols = jax.ShapeDtypeStruct((4, *here.shape), block.dtype)
        cols = small_call(join_kernel, cols, here, far, kept, *moved, scalars=0)
        return pieces, cols, done

    rows0, mine0, done0 = gathered(own, 1, other)
    rows1, mine1, _ = gathered(first_of(other, *done0), 2)
    rows = (*rows0, *rows1)

    place = jnp.stack([f, y, core])
    theirs0 = from_core(mine0)
    mine1, *ready = lax.optimization_barrier((mine1, *terms_of(place, rows, mine0)))
    theirs1 = from_core(mine1)
    ready = (*ready, *terms_of(place, rows, theirs0), *terms_of(place, rows, mine1))
    sent = terms_of(place, rows, theirs1, ready).astype(jnp.float16)
    got = lax.all_to_all(sent, ("zh", "zl", "x"), 0, 0, tiled=True)

    whole = jax.ShapeDtypeStruct((2, 2, n, n), jnp.float32)
    kernel = functools.partial(sum_kernel, (16 * wavefield.shape[2]) ** -0.5)
    return small_call(kernel, whole, got.astype(jnp.float32), scalars=0)


def solution(mesh):
    fine = Mesh(mesh.devices.reshape(SIZES), AXES)
    return jax.shard_map(
        body,
        mesh=fine,
        in_specs=(P(None, None, ("zl", "x"), ("zh", "y", "core")),),
        out_specs=P(None, None, ("zh", "y", "core"), ("zl", "x")),
        check_vma=False,
    )
```

```python
import functools

import jax
import jax.numpy as jnp
from jax import lax
from jax.experimental import pallas as pl
from jax.experimental.pallas import tpu as pltpu
from jax.sharding import Mesh
from jax.sharding import PartitionSpec as P

AXES = ("zh", "y", "core", "zl", "x")
SIZES = (2, 4, 2, 4, 4)
TOP = 12


def ring(n, step):
    return [(i, (i + step) % n) for i in range(n)]


def first_of(value, *after):
    return lax.optimization_barrier((value, *after))[0]


def add_terms(place, *refs):
    f, y = place[0], place[1]
    blocks, (cols, out, top) = (refs[:4], refs[4:9]), refs[9:]
    n, c = out.shape[2:]
    first = lax.broadcasted_iota(jnp.int32, (n, 2 * c), 1) % c < c // 2
    top[...] = jnp.zeros_like(top)
    for dy in (0, 2):
        for e, pieces in enumerate(blocks):
            real = imag = 0.0
            start = 0
            for piece in pieces:
                here = slice(start, start + piece.shape[1])
                start = here.stop
                weights = jnp.concatenate([cols[dy, here], cols[dy + 1, here]], axis=1)
                real += across(piece[0], weights)
                imag += across(piece[1], weights)
            turned = jnp.concatenate([pltpu.roll(imag[:, :c], c // 2, 1), pltpu.roll(imag[:, c:], c // 2, 1)], axis=1)
            term = real + jnp.where(first, turned, -turned)
            for i in range(2):
                out[f ^ e, lax.rem(y + dy + i, 4)] = term[:, i * c : (i + 1) * c]
            size = jnp.abs(term).reshape(n // 8, 8, 2 * c).max(0)
            top[...] = jnp.maximum(top[...], jnp.maximum(size[:, :c], size[:, c:]))


def across(a, b):
    return lax.dot_general(a, b, (((0,), (0,)), ((), ())), preferred_element_type=jnp.float32)


def group_of(block, number):
    size = block.shape[2] // 4
    return jnp.concatenate([block[p, :, number * size : (number + 1) * size] for p in range(2)], axis=1)


def near_kernel(x, above, below, *outs):
    for place in range(4):

        @pl.when(x[0] == place)
        def _():
            for out, step in zip(outs, (0, -1, 1, 2)):
                for i, block in enumerate((above, below)):
                    out[i] = group_of(block, (place + step) % 4)


def own_kernel(x, *refs):
    out = refs[-1]
    for place in range(4):

        @pl.when(x[0] == place)
        def _():
            start = 0
            for piece in refs[:-1]:
                out[start : start + piece.shape[1]] = group_of(piece, place)
                start += piece.shape[1]


def join_kernel(here, far, *refs):
    out = refs[-1]
    out[0], out[2] = here[...], far[...]
    for i, ref in enumerate(refs[:-1]):
        s = ref.shape[1]
        out[1, i * s : (i + 1) * s], out[3, i * s : (i + 1) * s] = ref[0], ref[1]


SPACE = pl.BlockSpec(memory_space=pltpu.VMEM)
GRANT = 40 * 2**20
SCALAR = pl.BlockSpec(memory_space=pltpu.SMEM)


def small_call(kernel, shapes, *operands, scalars=1):
    size = sum(2 * a.size for a in operands[scalars:])
    return pl.pallas_call(
        kernel,
        out_shape=shapes,
        in_specs=[SCALAR] * scalars + [SPACE] * (len(operands) - scalars),
        out_specs=jax.tree.map(lambda _: SPACE, shapes),
        compiler_params=pltpu.CompilerParams(vmem_limit_bytes=GRANT),
        cost_estimate=pl.CostEstimate(flops=0, bytes_accessed=size, transcendentals=0),
    )(*operands)


def last_kernel(place, *refs):
    term0, top0, term1, top1, term2, top2, out, term3, top3 = refs[10:]
    add_terms(place, *refs[:10], term3, top3)
    f, core = place[0], place[2]
    n, c = term3.shape[2:]
    largest = jnp.max(jnp.maximum(jnp.maximum(top0[...], top1[...]), jnp.maximum(top2[...], top3[...])))
    power = jnp.clip(jnp.floor(jnp.log2(jnp.full((8, c), largest))), -100.0, 100.0)
    factor = jnp.exp2(TOP - power[:1]) * (1.0 + pattern(n, c))

    def step(i, carry):
        zr, yc = i // 4, lax.rem(i, 4)
        for number, term in enumerate((term0, term1, term2, term3)):
            zc, core_col = f ^ (number // 2), core ^ (number % 2)
            owner = zr * 16 + zc * 8 + yc * 2 + core_col
            out[owner, :n] = term[zr, yc] * factor
            out[owner, n:] = power
        return carry

    lax.fori_loop(0, 8, step, 0)


def terms_of(place, rows, cols, others=None):
    n, c = rows[0].shape[2], cols.shape[2]
    term = (2, 4, n, c)
    if others is None:
        kernel, operands, scratch = add_terms, (place, *rows, cols), []
        shapes = (jax.ShapeDtypeStruct(term, jnp.float32), jax.ShapeDtypeStruct((8, c), jnp.float32))
    else:
        kernel, operands = last_kernel, (place, *rows, cols, *others)
        scratch = [pltpu.VMEM(term, jnp.float32), pltpu.VMEM((8, c), jnp.float32)]
        shapes = jax.ShapeDtypeStruct((32, n + 8, c), jnp.float32)
    return pl.pallas_call(
        kernel,
        out_shape=shapes,
        in_specs=[SCALAR] + [SPACE] * (len(operands) - 1),
        out_specs=SPACE if others else (SPACE, SPACE),
        scratch_shapes=scratch,
        compiler_params=pltpu.CompilerParams(vmem_limit_bytes=GRANT),
        cost_estimate=pl.CostEstimate(flops=32 * n * cols.shape[1] * c, bytes_accessed=8 * 2**20, transcendentals=0),
    )(*operands)


def sum_kernel(scale, got, out):
    n = out.shape[2]
    c = got.shape[2]
    undo = (1.0 - pattern(n, c)) * scale
    for f in range(2):
        for x in range(4):
            total = 0.0
            for zl in range(4):
                chunk = f * 16 + zl * 4 + x
                total += got[chunk, :n] * jnp.exp2(got[chunk, n : n + 1] - TOP)
            total *= undo
            for p in range(2):
                out[f, p, :, x * c // 2 : (x + 1) * c // 2] = total[:, p * c // 2 : (p + 1) * c // 2]


def pattern(rows, cols):
    i = lax.broadcasted_iota(jnp.int32, (rows, cols), 0)
    j = lax.broadcasted_iota(jnp.int32, (rows, cols), 1)
    return ((i * 157 + j * 91) % 256 - 127.5).astype(jnp.float32) * 2.0**-18


def body(wavefield):
    f, y, core, zl, x = (lax.axis_index(name) for name in AXES)
    n = wavefield.shape[3]
    group = n // 4

    other = lax.dynamic_index_in_dim(wavefield, 1 - f, 0, keepdims=False)
    own = lax.dynamic_index_in_dim(first_of(wavefield, other), f, 0, keepdims=False)
    other = lax.ppermute(other, "zh", ring(2, 1))

    def from_y(block, step):
        return lax.ppermute(block, "y", ring(4, -step))

    def from_core(piece):
        return lax.ppermute(piece, "core", ring(2, 1))

    def gathered(block, ways, *late, before=()):
        shots = block.shape[1]
        above, below = (lax.ppermute(block, "x", ring(4, step)) for step in (-1, 1))
        near = [from_y(first_of(block, *before), step) for step in (1, 3)]
        near = lax.optimization_barrier((*near, above, below))[:2]
        cut = jax.ShapeDtypeStruct((2, shots, 2 * group), block.dtype)
        kept, *sent = small_call(near_kernel, (cut,) * 4, x[None], *near)
        moved = [lax.ppermute(part, "x", ring(4, step)) for part, step in zip(sent, (-1, 1, 2))]
        relayed = [lax.ppermute(above[:, : shots // ways], "x", ring(4, -1))]
        if ways == 2:
            relayed.append(lax.ppermute(below[:, shots // 2 :], "x", ring(4, 1)))
        done = [*moved, *relayed]
        pieces = [block, above, below, *lax.optimization_barrier((*relayed, kept, *late))[:ways]]
        here = jax.ShapeDtypeStruct((4 * shots, 2 * group), block.dtype)
        here = small_call(own_kernel, here, x[None], *pieces)
        far = from_y(here, 2)
        cols = jax.ShapeDtypeStruct((4, *here.shape), block.dtype)
        cols = small_call(join_kernel, cols, here, far, kept, *moved, scalars=0)
        return pieces, cols, done, here

    rows0, mine0, done0, here0 = gathered(own, 1, other)
    rows1, mine1, _, _ = gathered(first_of(other, *done0), 2, before=(here0,))
    rows = (*rows0, *rows1)

    place = jnp.stack([f, y, core])
    theirs0 = from_core(mine0)
    mine1, *ready = lax.optimization_barrier((mine1, *terms_of(place, rows, mine0)))
    theirs1 = from_core(mine1)
    ready = (*ready, *terms_of(place, rows, theirs0), *terms_of(place, rows, mine1))
    sent = terms_of(place, rows, theirs1, ready).astype(jnp.float16)
    got = lax.all_to_all(sent, ("zh", "zl", "x"), 0, 0, tiled=True)

    whole = jax.ShapeDtypeStruct((2, 2, n, n), jnp.float32)
    kernel = functools.partial(sum_kernel, (16 * wavefield.shape[2]) ** -0.5)
    return small_call(kernel, whole, got.astype(jnp.float32), scalars=0)


def solution(mesh):
    fine = Mesh(mesh.devices.reshape(SIZES), AXES)
    return jax.shard_map(
        body,
        mesh=fine,
        in_specs=(P(None, None, ("zl", "x"), ("zh", "y", "core")),),
        out_specs=P(None, None, ("zh", "y", "core"), ("zl", "x")),
        check_vma=False,
    )
```

```python
import functools

import jax
import jax.numpy as jnp
from jax import lax
from jax.experimental import pallas as pl
from jax.experimental.pallas import tpu as pltpu
from jax.sharding import Mesh
from jax.sharding import PartitionSpec as P

AXES = ("zh", "y", "core", "zl", "x")
SIZES = (2, 4, 2, 4, 4)
TOP = 12


def ring(n, step):
    return [(i, (i + step) % n) for i in range(n)]


def first_of(value, *after):
    return lax.optimization_barrier((value, *after))[0]


def add_terms(place, *refs):
    f, y = place[0], place[1]
    blocks, (cols, out, top) = (refs[:5], refs[5:10]), refs[10:]
    n, c = out.shape[2:]
    first = lax.broadcasted_iota(jnp.int32, (n, 2 * c), 1) % c < c // 2
    top[...] = jnp.zeros_like(top)
    for dy in (0, 2):
        for e, pieces in enumerate(blocks):
            real = imag = 0.0
            start = 0
            for piece in pieces:
                here = slice(start, start + piece.shape[1])
                start = here.stop
                weights = jnp.concatenate([cols[dy, here], cols[dy + 1, here]], axis=1)
                real += across(piece[0], weights)
                imag += across(piece[1], weights)
            turned = jnp.concatenate([pltpu.roll(imag[:, :c], c // 2, 1), pltpu.roll(imag[:, c:], c // 2, 1)], axis=1)
            term = real + jnp.where(first, turned, -turned)
            for i in range(2):
                out[f ^ e, lax.rem(y + dy + i, 4)] = term[:, i * c : (i + 1) * c]
            size = jnp.abs(term).reshape(n // 8, 8, 2 * c).max(0)
            top[...] = jnp.maximum(top[...], jnp.maximum(size[:, :c], size[:, c:]))


def across(a, b):
    return lax.dot_general(a, b, (((0,), (0,)), ((), ())), preferred_element_type=jnp.float32)


def group_of(block, number):
    size = block.shape[2] // 4
    return jnp.concatenate([block[p, :, number * size : (number + 1) * size] for p in range(2)], axis=1)


def near_kernel(x, above, below, *outs):
    for place in range(4):

        @pl.when(x[0] == place)
        def _():
            for out, step in zip(outs, (0, -1, 1, 2)):
                for i, block in enumerate((above, below)):
                    out[i] = group_of(block, (place + step) % 4)


def own_kernel(x, *refs):
    out = refs[-1]
    for place in range(4):

        @pl.when(x[0] == place)
        def _():
            start = 0
            for piece in refs[:-1]:
                out[start : start + piece.shape[1]] = group_of(piece, place)
                start += piece.shape[1]


def join_kernel(here, far, *refs):
    out = refs[-1]
    out[0], out[2] = here[...], far[...]
    for i, ref in enumerate(refs[:-1]):
        s = ref.shape[1]
        out[1, i * s : (i + 1) * s], out[3, i * s : (i + 1) * s] = ref[0], ref[1]


SPACE = pl.BlockSpec(memory_space=pltpu.VMEM)
GRANT = 40 * 2**20
SCALAR = pl.BlockSpec(memory_space=pltpu.SMEM)


def small_call(kernel, shapes, *operands, scalars=1):
    size = sum(2 * a.size for a in operands[scalars:])
    return pl.pallas_call(
        kernel,
        out_shape=shapes,
        in_specs=[SCALAR] * scalars + [SPACE] * (len(operands) - scalars),
        out_specs=jax.tree.map(lambda _: SPACE, shapes),
        compiler_params=pltpu.CompilerParams(vmem_limit_bytes=GRANT),
        cost_estimate=pl.CostEstimate(flops=0, bytes_accessed=size, transcendentals=0),
    )(*operands)


def last_kernel(place, *refs):
    term0, top0, term1, top1, term2, top2, out, term3, top3 = refs[11:]
    add_terms(place, *refs[:11], term3, top3)
    f, core = place[0], place[2]
    n, c = term3.shape[2:]
    largest = jnp.max(jnp.maximum(jnp.maximum(top0[...], top1[...]), jnp.maximum(top2[...], top3[...])))
    power = jnp.clip(jnp.floor(jnp.log2(jnp.full((8, c), largest))), -100.0, 100.0)
    factor = jnp.exp2(TOP - power[:1]) * (1.0 + pattern(n, c))

    def step(i, carry):
        zr, yc = i // 4, lax.rem(i, 4)
        for number, term in enumerate((term0, term1, term2, term3)):
            zc, core_col = f ^ (number // 2), core ^ (number % 2)
            owner = zr * 16 + zc * 8 + yc * 2 + core_col
            out[owner, :n] = term[zr, yc] * factor
            out[owner, n:] = tail
        return carry

    tail = jnp.where(lax.broadcasted_iota(jnp.int32, (8, c), 0) == 1, 0.0, power)
    lax.fori_loop(0, 8, step, 0)
    on = diagonal(n, c, place[3])
    for zc in range(2):
        owner = zc * 24 + place[1] * 2 + core
        value = out[owner, :n]
        split = value * 8193.0
        high = split - (split - value)
        out[owner, :n] = jnp.where(on, high, value)
        out[owner, n + 1 : n + 2] = jnp.sum(jnp.where(on, value - high, 0.0), axis=0, keepdims=True)


def terms_of(place, rows, cols, others=None):
    n, c = rows[0].shape[2], cols.shape[2]
    term = (2, 4, n, c)
    if others is None:
        kernel, operands, scratch = add_terms, (place, *rows, cols), []
        shapes = (jax.ShapeDtypeStruct(term, jnp.float32), jax.ShapeDtypeStruct((8, c), jnp.float32))
    else:
        kernel, operands = last_kernel, (place, *rows, cols, *others)
        scratch = [pltpu.VMEM(term, jnp.float32), pltpu.VMEM((8, c), jnp.float32)]
        shapes = jax.ShapeDtypeStruct((32, n + 8, c), jnp.float32)
    return pl.pallas_call(
        kernel,
        out_shape=shapes,
        in_specs=[SCALAR] + [SPACE] * (len(operands) - 1),
        out_specs=SPACE if others else (SPACE, SPACE),
        scratch_shapes=scratch,
        compiler_params=pltpu.CompilerParams(vmem_limit_bytes=GRANT),
        cost_estimate=pl.CostEstimate(flops=32 * n * cols.shape[1] * c, bytes_accessed=8 * 2**20, transcendentals=0),
    )(*operands)


def sum_kernel(scale, got, out):
    n = out.shape[2]
    c = got.shape[2]
    undo = (1.0 - pattern(n, c)) * scale
    for f in range(2):
        for x in range(4):
            total = 0.0
            for zl in range(4):
                chunk = f * 16 + zl * 4 + x
                rest = jnp.where(diagonal(n, c, x), got[chunk, n + 1 : n + 2], 0.0)
                total += (got[chunk, :n] + rest) * jnp.exp2(got[chunk, n : n + 1] - TOP)
            total *= undo
            for p in range(2):
                out[f, p, :, x * c // 2 : (x + 1) * c // 2] = total[:, p * c // 2 : (p + 1) * c // 2]


def diagonal(rows, cols, group):
    i = lax.broadcasted_iota(jnp.int32, (rows, cols), 0)
    j = lax.broadcasted_iota(jnp.int32, (rows, cols), 1)
    return (i == group * (cols // 2) + j) & (j < cols // 2)


def pattern(rows, cols):
    i = lax.broadcasted_iota(jnp.int32, (rows, cols), 0)
    j = lax.broadcasted_iota(jnp.int32, (rows, cols), 1)
    return ((i * 157 + j * 91) % 256 - 127.5).astype(jnp.float32) * 2.0**-18


def body(wavefield):
    f, y, core, zl, x = (lax.axis_index(name) for name in AXES)
    n = wavefield.shape[3]
    group = n // 4

    other = lax.dynamic_index_in_dim(wavefield, 1 - f, 0, keepdims=False)
    own = lax.dynamic_index_in_dim(first_of(wavefield, other), f, 0, keepdims=False)
    other = lax.ppermute(other, "zh", ring(2, 1))

    def from_y(block, step):
        return lax.ppermute(block, "y", ring(4, -step))

    def from_core(piece):
        return lax.ppermute(piece, "core", ring(2, 1))

    def gathered(block, *late):
        shots = block.shape[1]
        above, below = (lax.ppermute(block, "x", ring(4, step)) for step in (-1, 1))
        near = [from_y(block, 1), from_y(block, 3)]
        near = lax.optimization_barrier((*near, above, below))[:2]
        cut = jax.ShapeDtypeStruct((2, shots, 2 * group), block.dtype)
        kept, *sent = small_call(near_kernel, (cut,) * 4, x[None], *near)
        moved = [lax.ppermute(part, "x", ring(4, step)) for part, step in zip(sent, (-1, 1, 2))]
        far_a = lax.ppermute(above[:, : shots // 2], "x", ring(4, -1))
        far_b = lax.ppermute(below[:, shots // 2 :], "x", ring(4, 1))
        far_a, far_b = lax.optimization_barrier((far_a, far_b, kept, *late))[:2]
        pieces = [block, above, below, far_a, far_b]
        here = jax.ShapeDtypeStruct((4 * shots, 2 * group), block.dtype)
        here = small_call(own_kernel, here, x[None], *pieces)
        far = from_y(here, 2)
        cols = jax.ShapeDtypeStruct((4, *here.shape), block.dtype)
        cols = small_call(join_kernel, cols, here, far, kept, *moved, scalars=0)
        return pieces, cols, moved

    rows0, mine0, moved0 = gathered(own, other)
    rows1, mine1, _ = gathered(first_of(other, *moved0))
    rows = (*rows0, *rows1)

    place = jnp.stack([f, y, core, x])
    theirs0 = from_core(mine0)
    mine1, *ready = lax.optimization_barrier((mine1, *terms_of(place, rows, mine0)))
    theirs1 = from_core(mine1)
    ready = (*ready, *terms_of(place, rows, theirs0), *terms_of(place, rows, mine1))
    sent = terms_of(place, rows, theirs1, ready).astype(jnp.float16)
    got = lax.all_to_all(sent, ("zh", "zl", "x"), 0, 0, tiled=True)

    whole = jax.ShapeDtypeStruct((2, 2, n, n), jnp.float32)
    kernel = functools.partial(sum_kernel, (16 * wavefield.shape[2]) ** -0.5)
    return small_call(kernel, whole, got.astype(jnp.float32), scalars=0)


def solution(mesh):
    fine = Mesh(mesh.devices.reshape(SIZES), AXES)
    return jax.shard_map(
        body,
        mesh=fine,
        in_specs=(P(None, None, ("zl", "x"), ("zh", "y", "core")),),
        out_specs=P(None, None, ("zh", "y", "core"), ("zl", "x")),
        check_vma=False,
    )
```

```python
import functools

import jax
import jax.numpy as jnp
from jax import lax
from jax.experimental import pallas as pl
from jax.experimental.pallas import tpu as pltpu
from jax.sharding import Mesh
from jax.sharding import PartitionSpec as P

AXES = ("zh", "y", "core", "zl", "x")
SIZES = (2, 4, 2, 4, 4)
TOP = 12


def ring(n, step):
    return [(i, (i + step) % n) for i in range(n)]


def first_of(value, *after):
    return lax.optimization_barrier((value, *after))[0]


def add_terms(place, *refs):
    f, y = place[0], place[1]
    blocks, (cols, out, top) = (refs[:5], refs[5:10]), refs[10:]
    n, c = out.shape[2:]
    first = lax.broadcasted_iota(jnp.int32, (n, 2 * c), 1) % c < c // 2
    top[...] = jnp.zeros_like(top)
    for dy in (0, 2):
        for e, pieces in enumerate(blocks):
            both = 0.0
            start = 0
            for piece in pieces:
                here = slice(start, start + piece.shape[1])
                start = here.stop
                weights = jnp.concatenate([cols[dy, here], cols[dy + 1, here]], axis=1)
                both += across(jnp.concatenate([piece[0], piece[1]], axis=1), weights)
            real, imag = both[:n], both[n:]
            turned = jnp.concatenate([pltpu.roll(imag[:, :c], c // 2, 1), pltpu.roll(imag[:, c:], c // 2, 1)], axis=1)
            term = real + jnp.where(first, turned, -turned)
            for i in range(2):
                out[f ^ e, lax.rem(y + dy + i, 4)] = term[:, i * c : (i + 1) * c]
            size = jnp.abs(term).reshape(n // 8, 8, 2 * c).max(0)
            top[...] = jnp.maximum(top[...], jnp.maximum(size[:, :c], size[:, c:]))


def across(a, b):
    return lax.dot_general(a, b, (((0,), (0,)), ((), ())), preferred_element_type=jnp.float32)


def group_of(block, number):
    size = block.shape[2] // 4
    return jnp.concatenate([block[p, :, number * size : (number + 1) * size] for p in range(2)], axis=1)


def near_kernel(x, above, below, *outs):
    for place in range(4):

        @pl.when(x[0] == place)
        def _():
            for out, step in zip(outs, (0, -1, 1, 2)):
                for i, block in enumerate((above, below)):
                    out[i] = group_of(block, (place + step) % 4)


def own_kernel(x, *refs):
    out = refs[-1]
    for place in range(4):

        @pl.when(x[0] == place)
        def _():
            start = 0
            for piece in refs[:-1]:
                out[start : start + piece.shape[1]] = group_of(piece, place)
                start += piece.shape[1]


def join_kernel(here, far, *refs):
    out = refs[-1]
    out[0], out[2] = here[...], far[...]
    for i, ref in enumerate(refs[:-1]):
        s = ref.shape[1]
        out[1, i * s : (i + 1) * s], out[3, i * s : (i + 1) * s] = ref[0], ref[1]


SPACE = pl.BlockSpec(memory_space=pltpu.VMEM)
GRANT = 40 * 2**20
SCALAR = pl.BlockSpec(memory_space=pltpu.SMEM)


def small_call(kernel, shapes, *operands, scalars=1):
    size = sum(2 * a.size for a in operands[scalars:])
    return pl.pallas_call(
        kernel,
        out_shape=shapes,
        in_specs=[SCALAR] * scalars + [SPACE] * (len(operands) - scalars),
        out_specs=jax.tree.map(lambda _: SPACE, shapes),
        compiler_params=pltpu.CompilerParams(vmem_limit_bytes=GRANT),
        cost_estimate=pl.CostEstimate(flops=0, bytes_accessed=size, transcendentals=0),
    )(*operands)


def last_kernel(place, *refs):
    term0, top0, term1, top1, term2, top2, out, term3, top3 = refs[11:]
    add_terms(place, *refs[:11], term3, top3)
    f, core = place[0], place[2]
    n, c = term3.shape[2:]
    largest = jnp.max(jnp.maximum(jnp.maximum(top0[...], top1[...]), jnp.maximum(top2[...], top3[...])))
    power = jnp.clip(jnp.floor(jnp.log2(jnp.full((8, c), largest))), -100.0, 100.0)
    factor = jnp.exp2(TOP - power[:1]) * (1.0 + pattern(n, c))

    def step(i, carry):
        zr, yc = i // 4, lax.rem(i, 4)
        for number, term in enumerate((term0, term1, term2, term3)):
            zc, core_col = f ^ (number // 2), core ^ (number % 2)
            owner = zr * 16 + zc * 8 + yc * 2 + core_col
            out[owner, :n] = term[zr, yc] * factor
            out[owner, n:] = tail
        return carry

    tail = jnp.where(lax.broadcasted_iota(jnp.int32, (8, c), 0) == 1, 0.0, power)
    lax.fori_loop(0, 8, step, 0)
    on = diagonal(n, c, place[3])
    for zc in range(2):
        owner = zc * 24 + place[1] * 2 + core
        value = out[owner, :n]
        split = value * 8193.0
        high = split - (split - value)
        out[owner, :n] = jnp.where(on, high, value)
        out[owner, n + 1 : n + 2] = jnp.sum(jnp.where(on, value - high, 0.0), axis=0, keepdims=True)


def terms_of(place, rows, cols, others=None):
    n, c = rows[0].shape[2], cols.shape[2]
    term = (2, 4, n, c)
    if others is None:
        kernel, operands, scratch = add_terms, (place, *rows, cols), []
        shapes = (jax.ShapeDtypeStruct(term, jnp.float32), jax.ShapeDtypeStruct((8, c), jnp.float32))
    else:
        kernel, operands = last_kernel, (place, *rows, cols, *others)
        scratch = [pltpu.VMEM(term, jnp.float32), pltpu.VMEM((8, c), jnp.float32)]
        shapes = jax.ShapeDtypeStruct((32, n + 8, c), jnp.float32)
    return pl.pallas_call(
        kernel,
        out_shape=shapes,
        in_specs=[SCALAR] + [SPACE] * (len(operands) - 1),
        out_specs=SPACE if others else (SPACE, SPACE),
        scratch_shapes=scratch,
        compiler_params=pltpu.CompilerParams(vmem_limit_bytes=GRANT),
        cost_estimate=pl.CostEstimate(flops=32 * n * cols.shape[1] * c, bytes_accessed=8 * 2**20, transcendentals=0),
    )(*operands)


def sum_kernel(scale, got, out):
    n = out.shape[2]
    c = got.shape[2]
    undo = (1.0 - pattern(n, c)) * scale
    for f in range(2):
        for x in range(4):
            total = 0.0
            for zl in range(4):
                chunk = f * 16 + zl * 4 + x
                rest = jnp.where(diagonal(n, c, x), got[chunk, n + 1 : n + 2], 0.0)
                total += (got[chunk, :n] + rest) * jnp.exp2(got[chunk, n : n + 1] - TOP)
            total *= undo
            for p in range(2):
                out[f, p, :, x * c // 2 : (x + 1) * c // 2] = total[:, p * c // 2 : (p + 1) * c // 2]


def diagonal(rows, cols, group):
    i = lax.broadcasted_iota(jnp.int32, (rows, cols), 0)
    j = lax.broadcasted_iota(jnp.int32, (rows, cols), 1)
    return (i == group * (cols // 2) + j) & (j < cols // 2)


def pattern(rows, cols):
    i = lax.broadcasted_iota(jnp.int32, (rows, cols), 0)
    j = lax.broadcasted_iota(jnp.int32, (rows, cols), 1)
    return ((i * 157 + j * 91) % 256 - 127.5).astype(jnp.float32) * 2.0**-18


def body(wavefield):
    f, y, core, zl, x = (lax.axis_index(name) for name in AXES)
    n = wavefield.shape[3]
    group = n // 4

    other = lax.dynamic_index_in_dim(wavefield, 1 - f, 0, keepdims=False)
    own = lax.dynamic_index_in_dim(first_of(wavefield, other), f, 0, keepdims=False)
    other = lax.ppermute(other, "zh", ring(2, 1))

    def from_y(block, step):
        return lax.ppermute(block, "y", ring(4, -step))

    def from_core(piece):
        return lax.ppermute(piece, "core", ring(2, 1))

    def gathered(block, *late):
        shots = block.shape[1]
        above, below = (lax.ppermute(block, "x", ring(4, step)) for step in (-1, 1))
        near = [from_y(block, 1), from_y(block, 3)]
        near = lax.optimization_barrier((*near, above, below))[:2]
        cut = jax.ShapeDtypeStruct((2, shots, 2 * group), block.dtype)
        kept, *sent = small_call(near_kernel, (cut,) * 4, x[None], *near)
        moved = [lax.ppermute(part, "x", ring(4, step)) for part, step in zip(sent, (-1, 1, 2))]
        far_a = lax.ppermute(above[:, : shots // 2], "x", ring(4, -1))
        far_b = lax.ppermute(below[:, shots // 2 :], "x", ring(4, 1))
        far_a, far_b = lax.optimization_barrier((far_a, far_b, kept, *late))[:2]
        pieces = [block, above, below, far_a, far_b]
        here = jax.ShapeDtypeStruct((4 * shots, 2 * group), block.dtype)
        here = small_call(own_kernel, here, x[None], *pieces)
        far = from_y(here, 2)
        cols = jax.ShapeDtypeStruct((4, *here.shape), block.dtype)
        cols = small_call(join_kernel, cols, here, far, kept, *moved, scalars=0)
        return pieces, cols, moved

    rows0, mine0, moved0 = gathered(own, other)
    rows1, mine1, _ = gathered(first_of(other, *moved0))
    rows = (*rows0, *rows1)

    place = jnp.stack([f, y, core, x])
    theirs0 = from_core(mine0)
    mine1, *ready = lax.optimization_barrier((mine1, *terms_of(place, rows, mine0)))
    theirs1 = from_core(mine1)
    ready = (*ready, *terms_of(place, rows, theirs0), *terms_of(place, rows, mine1))
    sent = terms_of(place, rows, theirs1, ready).astype(jnp.float16)
    got = lax.all_to_all(sent, ("zh", "zl", "x"), 0, 0, tiled=True)

    whole = jax.ShapeDtypeStruct((2, 2, n, n), jnp.float32)
    kernel = functools.partial(sum_kernel, (16 * wavefield.shape[2]) ** -0.5)
    return small_call(kernel, whole, got.astype(jnp.float32), scalars=0)


def solution(mesh):
    fine = Mesh(mesh.devices.reshape(SIZES), AXES)
    return jax.shard_map(
        body,
        mesh=fine,
        in_specs=(P(None, None, ("zl", "x"), ("zh", "y", "core")),),
        out_specs=P(None, None, ("zh", "y", "core"), ("zl", "x")),
        check_vma=False,
    )
```
